32 devices in a mesh: dp: 16 (over z, y, x), tile: 2 (over core).
Axes of the slice: x: 2, y: 2, z: 4, core: 2. Of those that a mesh axis runs over, the one named last changes fastest.
Arguments:
- feats: bfloat16 [1024, 2048], P('dp'), may hold values from -11 to 11
- jitter: bfloat16 [1024, 2048], P('dp'), may hold values from -1.5 to 1.5
- mask_ids: int32 [1024, 2], P('dp'), may hold values from 0 to 31
- proj_weight: bfloat16 [2048, 4096], P('dp', 'tile'), may hold values from -0.125 to 0.125
Outputs:
- feats_grad: float32 [1024, 2048], P('dp', 'tile')
- diag_corr: float32 [4096], P('tile')
- cross_power: float32 [], replicated
The draws below stay inside these ranges and needn't reach their ends.
All inputs are finite; a program needn't handle non-finite values.
Results may differ from the reference program's by a relative error of at most 0.02.
Values may be sent and summed in bfloat16 or wider, within the bound.
A program may use at most 64 MiB of HBM per device.

```python
import jax
import jax.numpy as jnp
from jax import lax

D_IN = 2048
EMB = 4096
GROUPS = 32
BATCH = 1024


def draw_feats(key, part):
    first, second = jax.random.split(key, 2)
    positions = jnp.arange(BATCH, dtype=jnp.float32)
    rising = 0.6 * jnp.exp(jnp.log(3.0) * positions / BATCH)
    spread = jnp.exp(jax.random.uniform(second, (BATCH,), minval=-0.35, maxval=0.35))
    scales = (rising * spread)[:, None]
    values = jnp.clip(jax.random.normal(first, (BATCH, D_IN)), -4.0, 4.0) * scales
    return values.astype(jnp.bfloat16)


def place_ends(entries, rng, smallest, high):
    longest = entries.shape.index(max(entries.shape))
    spots = []
    for shift in (0, 1):
        where = [jax.random.randint(jax.random.fold_in(rng, axis), (), 0, length) for axis, length in enumerate(entries.shape)]
        where[longest] = (where[longest] + shift) % entries.shape[longest]
        spots.append(tuple(where))
    return entries.at[spots[0]].set(smallest).at[spots[1]].set(high)


def block_scale(rng, extent, shards, least, high):
    loudness, own = 1.0, jax.random.fold_in(rng, 6)
    for dim, blocks in shards:
        steps = jnp.exp(jax.random.uniform(jax.random.fold_in(own, dim), (blocks,), jnp.float32, least / len(shards), high / len(shards)))
        loudness = loudness * jnp.repeat(steps, extent[dim] // blocks).reshape([-1 if axis == dim else 1 for axis in range(len(extent))])
    return loudness


def scatter_about(key, dims, deviation, bound, shards=(), kind=jnp.bfloat16):
    array = deviation * jax.random.normal(key, dims, jnp.float32)
    if shards:
        array = array * block_scale(key, dims, shards, -0.22, 0.18)
    return jnp.clip(array, -bound, bound).astype(kind)


def setup_inputs(seed: int = 0) -> dict:
    key_of = jax.random.split(jax.random.key(seed), 5)
    return {
        "feats": draw_feats(jax.random.fold_in(key_of[4], 71), 0),
        "jitter": scatter_about(key_of[1], (BATCH, D_IN), 0.25, 1.5, ((0, 16),)),
        "mask_ids": place_ends(jax.random.randint(key_of[2], (BATCH, 2), 0, GROUPS), jax.random.fold_in(key_of[2], 1), 0, GROUPS - 1).astype(jnp.int32),
        "proj_weight": scatter_about(key_of[3], (D_IN, EMB), D_IN ** -0.5, 0.125, ((0, 16), (1, 2))),
    }


LAMBDA_OFF = 0.0051
NORM_EPS = 1e-05
LOSS_SCALE = 65536.0

def reference(feats, jitter, mask_ids, proj_weight):
    group_size = D_IN // GROUPS
    channel_group = jnp.arange(D_IN, dtype=jnp.int32)[None, :] // group_size
    keep_a = (channel_group != mask_ids[:, 0:1]).astype(jnp.float32)
    keep_b = (channel_group != mask_ids[:, 1:2]).astype(jnp.float32)
    view_a = (feats.astype(jnp.float32) * keep_a).astype(jnp.bfloat16)
    view_b = (feats.astype(jnp.float32) * keep_b + jitter.astype(jnp.float32)).astype(jnp.bfloat16)

    def project(view):
        raw = jnp.dot(view, proj_weight, preferred_element_type=jnp.float32).astype(jnp.bfloat16)
        values = raw.astype(jnp.float32)
        mean = lax.optimization_barrier(jnp.mean(values, axis=0))
        centered = values - mean
        inverse = lax.rsqrt(lax.optimization_barrier(jnp.mean(centered * centered, axis=0)) + NORM_EPS)
        return ((centered * inverse).astype(jnp.bfloat16), inverse)
    norm_a, inv_a = project(view_a)
    norm_b, inv_b = project(view_b)
    za = norm_a.astype(jnp.float32)
    zb = norm_b.astype(jnp.float32)
    diag_corr = lax.optimization_barrier(jnp.sum(za * zb, axis=0)) / BATCH
    gram_a = jnp.dot(norm_a, norm_a.T, preferred_element_type=jnp.float32)
    gram_b = jnp.dot(norm_b, norm_b.T, preferred_element_type=jnp.float32)
    cross_power = jnp.sum(gram_a * gram_b) / (BATCH * BATCH) / EMB
    coeff = -2.0 * (1.0 - diag_corr) - 2.0 * LAMBDA_OFF * diag_corr
    factor = 2.0 * LAMBDA_OFF / (BATCH * BATCH)
    grad_na = zb * coeff / BATCH + factor * jnp.dot(gram_b.astype(jnp.bfloat16), norm_a, preferred_element_type=jnp.float32)
    grad_nb = za * coeff / BATCH + factor * jnp.dot(gram_a.astype(jnp.bfloat16), norm_b, preferred_element_type=jnp.float32)

    def norm_back(grad, normed, inverse):
        first = lax.optimization_barrier(jnp.mean(grad, axis=0))
        second = lax.optimization_barrier(jnp.mean(grad * normed, axis=0))
        return (inverse * (grad - first - normed * second)).astype(jnp.bfloat16)
    dz_a = norm_back(grad_na, za, inv_a)
    dz_b = norm_back(grad_nb, zb, inv_b)
    back_a = jnp.dot(dz_a, proj_weight.T, preferred_element_type=jnp.float32)
    back_b = jnp.dot(dz_b, proj_weight.T, preferred_element_type=jnp.float32)
    feats_grad = LOSS_SCALE * (keep_a * back_a + keep_b * back_b)
    return (feats_grad, diag_corr, cross_power)
```

```python
import functools
import itertools

import jax
import jax.numpy as jnp
from jax import lax
from jax.experimental import pallas as pl
from jax.experimental.pallas import tpu as pltpu
from jax.sharding import PartitionSpec as P

EMB = 4096
GROUPS = 32


LAMBDA_OFF = 0.0051
NORM_EPS = 1e-05
LOSS_SCALE = 65536.0


def masked_views(feats, jitter, mask_ids):
    width = feats.shape[1]
    group_size = width // GROUPS
    channel_group = lax.broadcasted_iota(jnp.int32, (1, width), 1) // group_size
    keep_a = (channel_group != mask_ids[:, 0:1]).astype(jnp.float32)
    keep_b = (channel_group != mask_ids[:, 1:2]).astype(jnp.float32)
    values = feats.astype(jnp.float32)
    view_a = (values * keep_a).astype(jnp.bfloat16)
    view_b = (values * keep_b + jitter.astype(jnp.float32)).astype(jnp.bfloat16)
    return (view_a, view_b, keep_a, keep_b)


def contract_last(left, right):
    return lax.dot_general(
        left, right, (((1,), (1,)), ((), ())), preferred_element_type=jnp.float32
    )


def on_device(feats, jitter, mask_ids, proj_weight):
    view_a, view_b, keep_a, keep_b = masked_views(feats, jitter, mask_ids)
    rows = feats.shape[0]
    total = rows * lax.axis_size("dp")
    piece = lax.all_gather(proj_weight, "dp", axis=0, tiled=True)
    raw_a = jnp.dot(view_a, piece, preferred_element_type=jnp.float32)
    raw_b = jnp.dot(view_b, piece, preferred_element_type=jnp.float32)
    raw_a = raw_a.astype(jnp.bfloat16)
    raw_b = raw_b.astype(jnp.bfloat16)
    values_a = raw_a.astype(jnp.float32)
    values_b = raw_b.astype(jnp.float32)
    moment_sums = lax.psum(
        (
            jnp.sum(values_a, axis=0),
            jnp.sum(values_a * values_a, axis=0),
            jnp.sum(values_b, axis=0),
            jnp.sum(values_b * values_b, axis=0),
        ),
        "dp",
    )
    mean_a = moment_sums[0] / total
    mean_b = moment_sums[2] / total
    inv_a = lax.rsqrt(moment_sums[1] / total - mean_a * mean_a + NORM_EPS)
    inv_b = lax.rsqrt(moment_sums[3] / total - mean_b * mean_b + NORM_EPS)
    norm_a = ((values_a - mean_a) * inv_a).astype(jnp.bfloat16)
    norm_b = ((values_b - mean_b) * inv_b).astype(jnp.bfloat16)
    outgoing_a, outgoing_b = (norm_a, norm_b)
    gathered_a, gathered_b = (
        lax.all_gather(outgoing_a, "dp", axis=0, tiled=True),
        lax.all_gather(outgoing_b, "dp", axis=0, tiled=True),
    )
    whole_a, whole_b = (gathered_a, gathered_b)
    za = norm_a.astype(jnp.float32)
    zb = norm_b.astype(jnp.float32)
    diag_corr = jnp.sum(whole_a.astype(jnp.float32) * whole_b.astype(jnp.float32), axis=0) / total
    gram_a, gram_b = (
        lax.psum(contract_last(norm_a, whole_a).astype(jnp.bfloat16), "tile").astype(jnp.float32),
        lax.psum(contract_last(norm_b, whole_b).astype(jnp.bfloat16), "tile").astype(jnp.float32),
    )
    trace_part = jnp.sum(gram_a * gram_b)
    gram_bf_a = gram_a.astype(jnp.bfloat16)
    gram_bf_b = gram_b.astype(jnp.bfloat16)
    coeff = -2.0 * (1.0 - diag_corr) - 2.0 * LAMBDA_OFF * diag_corr
    factor = 2.0 * LAMBDA_OFF / (total * total)
    grad_na = zb * coeff / total + factor * jnp.dot(
        gram_bf_b, whole_a, preferred_element_type=jnp.float32
    )
    grad_nb = za * coeff / total + factor * jnp.dot(
        gram_bf_a, whole_b, preferred_element_type=jnp.float32
    )
    sums = lax.psum(
        (
            jnp.sum(grad_na, axis=0),
            jnp.sum(grad_na * za, axis=0),
            jnp.sum(grad_nb, axis=0),
            jnp.sum(grad_nb * zb, axis=0),
            trace_part,
        ),
        "dp",
    )
    dz_a = (inv_a * (grad_na - sums[0] / total - za * (sums[1] / total))).astype(jnp.bfloat16)
    dz_b = (inv_b * (grad_nb - sums[2] / total - zb * (sums[3] / total))).astype(jnp.bfloat16)
    cross_power = sums[4] / (total * total) / EMB
    piece = lax.all_gather(proj_weight, "dp", axis=0, tiled=True)
    combined = keep_a * contract_last(dz_a, piece) + keep_b * contract_last(dz_b, piece)
    feats_grad = LOSS_SCALE * lax.psum_scatter(
        combined.astype(jnp.bfloat16), "tile", scatter_dimension=1, tiled=True
    ).astype(jnp.float32)
    return (feats_grad, diag_corr, cross_power)


ZS = 4
QS = 4
BF, F32 = jnp.bfloat16, jnp.float32


def fused_kernel(
    feats, jitter, mask, weight, out, diag_out, cross_out,
    views, ids, wbuf, raw, norm, gpart, gsib, gsend, grecv, gfull,
    small, sums, last, fsib_out, fsib, fown, fsend, frecv, send, recv, *, emb
):
    dp, t = lax.axis_index("dp"), lax.axis_index("tile")
    rows, width = feats.shape
    depth, local = weight.shape
    cols = local // ZS
    half = width // 2
    batch = rows * ZS * QS
    z, q = dp // QS, lax.rem(dp, QS)
    x, y = lax.rem(q, 2), q // 2
    sibling = (dp, 1 - t)
    beside_x = (dp + 1 - 2 * x, t)
    beside_y = (dp + 2 - 4 * y, t)
    across = (dp + 1 - 2 * x + 2 - 4 * y, t)
    q_x, q_y = q + 1 - 2 * x, q + 2 - 4 * y
    other_z = [lax.rem(z + d, ZS) for d in range(ZS)]
    from_z = [lax.rem(z + ZS - d, ZS) for d in range(ZS)]
    at_z = [(other_z[d] * QS + q, t) for d in range(ZS)]
    numbers = itertools.count()
    started = []

    def push(src, dst, device):
        i = next(numbers)
        copy = pltpu.make_async_remote_copy(
            src_ref=src, dst_ref=dst, send_sem=send.at[i], recv_sem=recv.at[i],
            device_id=device, device_id_type=pl.DeviceIdType.MESH,
        )
        copy.start()
        started.append(copy)
        return copy

    barrier = pltpu.get_barrier_semaphore()
    peers = [sibling, beside_x, beside_y, across] + at_z[1:]
    for peer in peers:
        pl.semaphore_signal(barrier, inc=1, device_id=peer, device_id_type=pl.DeviceIdType.MESH)
    pl.semaphore_wait(barrier, len(peers))

    def columns(d):
        return pl.ds(pl.multiple_of(other_z[d] * cols, 128), cols)

    w_z = {d: push(weight.at[:, columns(d)], wbuf.at[dp], at_z[d]) for d in (2, 1, 3)}
    wbuf[dp] = weight[:, columns(0)]

    group = lax.broadcasted_iota(jnp.int32, (rows, width), 1) // (width // GROUPS)
    keep_a, keep_b = (group != mask[:, 0:1]), (group != mask[:, 1:2])
    values = feats[...].astype(F32)
    own = pl.ds(pl.multiple_of(z * rows, rows), rows)
    views[0, own] = jnp.where(keep_a, values, 0.0).astype(BF)
    views[1, own] = (jnp.where(keep_b, values, 0.0) + jitter[...].astype(F32)).astype(BF)
    lanes = lax.broadcasted_iota(jnp.int32, (rows, 128), 1)
    ids[own] = jnp.where(lanes < 64, mask[:, 0:1], mask[:, 1:2]).astype(F32)

    def block(i):
        return pl.ds(pl.multiple_of(i * rows, rows), rows)

    mine = pl.ds(pl.multiple_of(t * half, 128), half)

    def spread_weight(zz):
        piece = wbuf.at[zz * QS + q]
        return push(piece, piece, beside_x), push(piece, piece, beside_y), zz

    first = [spread_weight(z)]
    v_z = {d: push(views.at[:, own, mine], views.at[:, own, mine], at_z[d]) for d in (2, 1, 3)}
    m_z = {d: push(ids.at[own], ids.at[own], at_z[d]) for d in (1, 2, 3)}
    for d in (1, 3, 2):
        w_z[d].wait_recv()
        first.append(spread_weight(from_z[d]))
    second = []
    for via_x, via_y, zz in first:
        via_x.wait_recv()
        piece = wbuf.at[zz * QS + q_x, pl.ds(0, depth // 2)]
        second.append(push(piece, piece, beside_y))
        via_y.wait_recv()
        piece = wbuf.at[zz * QS + q_y, pl.ds(depth // 2, depth // 2)]
        second.append(push(piece, piece, beside_x))
    v_s = []
    for d in (1, 3, 2):
        v_z[d].wait_recv()
        piece = views.at[:, block(from_z[d]), mine]
        v_s.append(push(piece, piece, sibling))
    for copy in second + v_s:
        copy.wait_recv()

    raw_copies = []
    for v in range(2):
        flat = wbuf[...].reshape(width, cols)
        raw[v, q] = jnp.dot(views[v], flat, preferred_element_type=F32).astype(BF)
        piece = raw.at[v, q]
        raw_copies.append((push(piece, piece, beside_x), push(piece, piece, beside_y)))
    many = ZS * rows
    second = []
    for v in range(2):
        raw_copies[v][0].wait_recv()
        piece = raw.at[v, q_x, pl.ds(0, many // 2)]
        second.append(push(piece, piece, beside_y))
        raw_copies[v][1].wait_recv()
        piece = raw.at[v, q_y, pl.ds(many // 2, many // 2)]
        second.append(push(piece, piece, beside_x))
    inverse = []
    for v in range(2):
        second[2 * v].wait_recv()
        second[2 * v + 1].wait_recv()
        total = jnp.zeros((1, cols), F32)
        for i in range(QS):
            total += jnp.sum(raw[v, i].astype(F32), axis=0, keepdims=True)
        mean = total / batch
        total = jnp.zeros((1, cols), F32)
        for i in range(QS):
            centered = raw[v, i].astype(F32) - mean
            total += jnp.sum(centered * centered, axis=0, keepdims=True)
        inv = lax.rsqrt(total / batch + NORM_EPS)
        inverse.append(inv)
        for i in range(QS):
            norm[v, i] = ((raw[v, i].astype(F32) - mean) * inv).astype(BF)
        gram = contract_last(norm[v, q], norm[v].reshape(batch, cols)).astype(BF)
        for i in range(ZS):
            for core in range(2):
                start = i * rows + core * (rows // 2)
                gpart[core, v, i] = gram[start : start + rows // 2]
    g_s = push(gpart.at[1 - t], gsib, sibling)
    total = jnp.zeros((1, cols), F32)
    for i in range(QS):
        total += jnp.sum(norm[0, i].astype(F32) * norm[1, i].astype(F32), axis=0, keepdims=True)
    diag = total / batch
    coeff = -2.0 * (1.0 - diag) - 2.0 * LAMBDA_OFF * diag
    g_s.wait_recv()
    g_z = {}
    for d in (2, 1, 3, 0):
        pair = gpart[t, :, other_z[d]].astype(F32) + gsib[:, other_z[d]].astype(F32)
        if d:
            gsend[d - 1] = pair.astype(BF)
            g_z[d] = push(gsend.at[d - 1], grecv.at[d - 1], at_z[d])
        else:
            gram = pair
    for d in (1, 3, 2):
        g_z[d].wait_recv()
        gram = gram + grecv[d - 1].astype(F32)
    gfull[z, t] = gram.astype(BF)
    piece = gfull.at[z, t]
    g_z = {d: push(piece, piece, at_z[d]) for d in (2, 1, 3)}
    g_s = [push(piece, piece, sibling)]
    power = jnp.sum(gram[0] * gram[1], keepdims=True)
    small[z] = jnp.concatenate(
        [diag, jnp.broadcast_to(power, (1, cols)), jnp.zeros((6, cols), F32)], axis=0
    )
    small_z = {d: push(small.at[z], small.at[z], at_z[d]) for d in (1, 2, 3)}
    for d in (1, 3, 2):
        g_z[d].wait_recv()
        piece = gfull.at[from_z[d], t]
        g_s.append(push(piece, piece, sibling))
    for copy in g_s:
        copy.wait_recv()

    factor = 2.0 * LAMBDA_OFF / (batch * batch)
    za, zb = norm[0, q].astype(F32), norm[1, q].astype(F32)
    gram_a = gfull[:, :, 0].reshape(many, batch)
    gram_b = gfull[:, :, 1].reshape(many, batch)
    grad_a = zb * (coeff / batch) + factor * jnp.dot(
        gram_b, norm[0].reshape(batch, cols), preferred_element_type=F32
    )
    grad_b = za * (coeff / batch) + factor * jnp.dot(
        gram_a, norm[1].reshape(batch, cols), preferred_element_type=F32
    )
    for d in (1, 2, 3):
        small_z[d].wait_recv()
    power = small[0, 1:2]
    for i in range(1, ZS):
        power = power + small[i, 1:2]
    parts = [grad_a, grad_a * za, grad_b, grad_b * zb]
    parts = [jnp.sum(part, axis=0, keepdims=True) for part in parts]
    sums[q] = jnp.concatenate(parts + [power, jnp.zeros((3, cols), F32)], axis=0)
    copies = [push(sums.at[q], sums.at[q], peer) for peer in (across, beside_x, beside_y)]
    for i in range(ZS):
        diag_out[0:1, i * cols : (i + 1) * cols] = small[i, 0:1]
    for copy in copies:
        copy.wait_recv()
    total = sums[0]
    for i in range(1, QS):
        total = total + sums[i]
    last[0] = total
    last_copy = push(last.at[0], last.at[1], sibling)
    mean = total / batch
    dz_a = (inverse[0] * (grad_a - mean[0:1] - za * mean[1:2])).astype(BF)
    dz_b = (inverse[1] * (grad_b - mean[2:3] - zb * mean[3:4])).astype(BF)

    for d in (1, 2, 3):
        m_z[d].wait_recv()

    def share(core):
        slabs = wbuf.shape[0] // 2
        part = wbuf[pl.ds(core * slabs, slabs)].reshape(half, cols)
        group = (lax.broadcasted_iota(jnp.int32, (1, half), 1) + core * half) // (width // GROUPS)
        group = group.astype(F32)
        back_a = jnp.where(group != ids[:, 0:1], contract_last(dz_a, part), 0.0)
        return back_a + jnp.where(group != ids[:, 64:65], contract_last(dz_b, part), 0.0)

    fsib_out[...] = share(1 - t).astype(BF).reshape(ZS, rows, half)
    f_s = push(fsib_out, fsib, sibling)
    fown[...] = share(t).reshape(ZS, rows, half)
    f_s.wait_recv()
    f_z = {}
    for d in (2, 1, 3, 0):
        pair = fown[other_z[d]] + fsib[other_z[d]].astype(F32)
        if d:
            fsend[d - 1] = pair.astype(BF)
            f_z[d] = push(fsend.at[d - 1], frecv.at[d - 1], at_z[d])
        else:
            result = pair
    last_copy.wait_recv()
    power = last[0, 4:5, 0:128] + last[1, 4:5, 0:128]
    cross_out[...] = jnp.broadcast_to(power, (8, 128)) / (batch * batch) / emb
    for d in (1, 3, 2):
        f_z[d].wait_recv()
        result = result + frecv[d - 1].astype(F32)
    out[...] = LOSS_SCALE * result
    for copy in started:
        copy.wait_send()


COPIES = 80


def fused(feats, jitter, mask_ids, proj_weight):
    rows, width = feats.shape
    depth, local = proj_weight.shape
    cols, half, many = local // ZS, width // 2, rows * ZS
    batch = many * QS
    vmem = pl.BlockSpec(memory_space=pltpu.VMEM)
    grad, diag, power = pl.pallas_call(
        functools.partial(fused_kernel, emb=EMB),
        out_shape=(
            jax.ShapeDtypeStruct((rows, half), F32),
            jax.ShapeDtypeStruct((1, local), F32),
            jax.ShapeDtypeStruct((8, 128), F32),
        ),
        in_specs=[vmem] * 4,
        out_specs=(vmem,) * 3,
        scratch_shapes=[
            pltpu.VMEM((2, many, width), BF),
            pltpu.VMEM((many, 128), F32),
            pltpu.VMEM((ZS * QS, depth, cols), BF),
            pltpu.VMEM((2, QS, many, cols), BF),
            pltpu.VMEM((2, QS, many, cols), BF),
            pltpu.VMEM((2, 2, ZS, rows // 2, batch), BF),
            pltpu.VMEM((2, ZS, rows // 2, batch), BF),
            pltpu.VMEM((ZS - 1, 2, rows // 2, batch), BF),
            pltpu.VMEM((ZS - 1, 2, rows // 2, batch), BF),
            pltpu.VMEM((ZS, 2, 2, rows // 2, batch), BF),
            pltpu.VMEM((ZS, 8, cols), F32),
            pltpu.VMEM((QS, 8, cols), F32),
            pltpu.VMEM((2, 8, cols), F32),
            pltpu.VMEM((ZS, rows, half), BF),
            pltpu.VMEM((ZS, rows, half), BF),
            pltpu.VMEM((ZS, rows, half), F32),
            pltpu.VMEM((ZS - 1, rows, half), BF),
            pltpu.VMEM((ZS - 1, rows, half), BF),
            pltpu.SemaphoreType.DMA((COPIES,)),
            pltpu.SemaphoreType.DMA((COPIES,)),
        ],
        compiler_params=pltpu.CompilerParams(
            collective_id=0, has_side_effects=True, vmem_limit_bytes=56 * 2**20
        ),
    )(feats, jitter, mask_ids, proj_weight)
    return grad, diag.reshape(local), power[0, 0]


def solution(mesh):
    in_specs = (P("dp", None), P("dp", None), P("dp", None), P("dp", "tile"))
    out_specs = (P("dp", "tile"), P("tile"), P())
    planes = mesh.shape["dp"] == ZS * QS and mesh.shape["tile"] == 2
    return jax.shard_map(
        fused if planes else on_device, mesh=mesh, in_specs=in_specs, out_specs=out_specs, check_vma=False
    )
```

```python
import functools
import itertools

import jax
import jax.numpy as jnp
from jax import lax
from jax.experimental import pallas as pl
from jax.experimental.pallas import tpu as pltpu
from jax.sharding import PartitionSpec as P

EMB = 4096
GROUPS = 32


LAMBDA_OFF = 0.0051
NORM_EPS = 1e-05
LOSS_SCALE = 65536.0


def masked_views(feats, jitter, mask_ids):
    width = feats.shape[1]
    group_size = width // GROUPS
    channel_group = lax.broadcasted_iota(jnp.int32, (1, width), 1) // group_size
    keep_a = (channel_group != mask_ids[:, 0:1]).astype(jnp.float32)
    keep_b = (channel_group != mask_ids[:, 1:2]).astype(jnp.float32)
    values = feats.astype(jnp.float32)
    view_a = (values * keep_a).astype(jnp.bfloat16)
    view_b = (values * keep_b + jitter.astype(jnp.float32)).astype(jnp.bfloat16)
    return (view_a, view_b, keep_a, keep_b)


def contract_last(left, right):
    return lax.dot_general(
        left, right, (((1,), (1,)), ((), ())), preferred_element_type=jnp.float32
    )


def on_device(feats, jitter, mask_ids, proj_weight):
    view_a, view_b, keep_a, keep_b = masked_views(feats, jitter, mask_ids)
    rows = feats.shape[0]
    total = rows * lax.axis_size("dp")
    piece = lax.all_gather(proj_weight, "dp", axis=0, tiled=True)
    raw_a = jnp.dot(view_a, piece, preferred_element_type=jnp.float32)
    raw_b = jnp.dot(view_b, piece, preferred_element_type=jnp.float32)
    raw_a = raw_a.astype(jnp.bfloat16)
    raw_b = raw_b.astype(jnp.bfloat16)
    values_a = raw_a.astype(jnp.float32)
    values_b = raw_b.astype(jnp.float32)
    moment_sums = lax.psum(
        (
            jnp.sum(values_a, axis=0),
            jnp.sum(values_a * values_a, axis=0),
            jnp.sum(values_b, axis=0),
            jnp.sum(values_b * values_b, axis=0),
        ),
        "dp",
    )
    mean_a = moment_sums[0] / total
    mean_b = moment_sums[2] / total
    inv_a = lax.rsqrt(moment_sums[1] / total - mean_a * mean_a + NORM_EPS)
    inv_b = lax.rsqrt(moment_sums[3] / total - mean_b * mean_b + NORM_EPS)
    norm_a = ((values_a - mean_a) * inv_a).astype(jnp.bfloat16)
    norm_b = ((values_b - mean_b) * inv_b).astype(jnp.bfloat16)
    outgoing_a, outgoing_b = (norm_a, norm_b)
    gathered_a, gathered_b = (
        lax.all_gather(outgoing_a, "dp", axis=0, tiled=True),
        lax.all_gather(outgoing_b, "dp", axis=0, tiled=True),
    )
    whole_a, whole_b = (gathered_a, gathered_b)
    za = norm_a.astype(jnp.float32)
    zb = norm_b.astype(jnp.float32)
    diag_corr = jnp.sum(whole_a.astype(jnp.float32) * whole_b.astype(jnp.float32), axis=0) / total
    gram_a, gram_b = (
        lax.psum(contract_last(norm_a, whole_a).astype(jnp.bfloat16), "tile").astype(jnp.float32),
        lax.psum(contract_last(norm_b, whole_b).astype(jnp.bfloat16), "tile").astype(jnp.float32),
    )
    trace_part = jnp.sum(gram_a * gram_b)
    gram_bf_a = gram_a.astype(jnp.bfloat16)
    gram_bf_b = gram_b.astype(jnp.bfloat16)
    coeff = -2.0 * (1.0 - diag_corr) - 2.0 * LAMBDA_OFF * diag_corr
    factor = 2.0 * LAMBDA_OFF / (total * total)
    grad_na = zb * coeff / total + factor * jnp.dot(
        gram_bf_b, whole_a, preferred_element_type=jnp.float32
    )
    grad_nb = za * coeff / total + factor * jnp.dot(
        gram_bf_a, whole_b, preferred_element_type=jnp.float32
    )
    sums = lax.psum(
        (
            jnp.sum(grad_na, axis=0),
            jnp.sum(grad_na * za, axis=0),
            jnp.sum(grad_nb, axis=0),
            jnp.sum(grad_nb * zb, axis=0),
            trace_part,
        ),
        "dp",
    )
    dz_a = (inv_a * (grad_na - sums[0] / total - za * (sums[1] / total))).astype(jnp.bfloat16)
    dz_b = (inv_b * (grad_nb - sums[2] / total - zb * (sums[3] / total))).astype(jnp.bfloat16)
    cross_power = sums[4] / (total * total) / EMB
    piece = lax.all_gather(proj_weight, "dp", axis=0, tiled=True)
    combined = keep_a * contract_last(dz_a, piece) + keep_b * contract_last(dz_b, piece)
    feats_grad = LOSS_SCALE * lax.psum_scatter(
        combined.astype(jnp.bfloat16), "tile", scatter_dimension=1, tiled=True
    ).astype(jnp.float32)
    return (feats_grad, diag_corr, cross_power)


ZS = 4
QS = 4
BF, F32 = jnp.bfloat16, jnp.float32


def fused_kernel(
    feats, jitter, mask, weight, out, diag_out, cross_out,
    views, ids, wbuf, raw, norm, gpart, gsib, gsend, grecv, gsum, gfull,
    stat, small, sums, last, fsib_out, fsib, fown, fsend, frecv, send, recv, *, emb
):
    dp, t = lax.axis_index("dp"), lax.axis_index("tile")
    rows, width = feats.shape
    depth, local = weight.shape
    cols = local // ZS
    half = width // 2
    batch = rows * ZS * QS
    z, q = dp // QS, lax.rem(dp, QS)
    x, y = lax.rem(q, 2), q // 2
    sibling = (dp, 1 - t)
    beside_x = (dp + 1 - 2 * x, t)
    beside_y = (dp + 2 - 4 * y, t)
    across = (dp + 1 - 2 * x + 2 - 4 * y, t)
    q_x, q_y = q + 1 - 2 * x, q + 2 - 4 * y
    other_z = [lax.rem(z + d, ZS) for d in range(ZS)]
    from_z = [lax.rem(z + ZS - d, ZS) for d in range(ZS)]
    at_z = [(other_z[d] * QS + q, t) for d in range(ZS)]
    numbers = itertools.count()
    started = []

    def push(src, dst, device):
        i = next(numbers)
        copy = pltpu.make_async_remote_copy(
            src_ref=src, dst_ref=dst, send_sem=send.at[i], recv_sem=recv.at[i],
            device_id=device, device_id_type=pl.DeviceIdType.MESH,
        )
        copy.start()
        started.append(copy)
        return copy

    barrier = pltpu.get_barrier_semaphore()
    peers = [sibling, beside_x, beside_y, across] + at_z[1:]
    for peer in peers:
        pl.semaphore_signal(barrier, inc=1, device_id=peer, device_id_type=pl.DeviceIdType.MESH)

    def block(i):
        return pl.ds(pl.multiple_of(i * rows, rows), rows)

    own = block(z)
    mine = pl.ds(pl.multiple_of(t * half, 128), half)

    square = [lax.broadcasted_iota(jnp.int32, (rows, rows), axis) for axis in range(2)]

    def id_column(v):
        row = jnp.broadcast_to(mask[v : v + 1, :].astype(F32), (rows, rows))
        return jnp.sum(jnp.where(square[0] == square[1], row, 0.0), axis=1, keepdims=True)

    id_a, id_b = id_column(0), id_column(1)
    group = lax.broadcasted_iota(jnp.int32, (1, width), 1) // (width // GROUPS)
    group = group.astype(F32)
    values = feats[...].astype(F32)
    views[0, own] = jnp.where(group != id_a, values, 0.0).astype(BF)
    views[1, own] = (jnp.where(group != id_b, values, 0.0) + jitter[...].astype(F32)).astype(BF)
    lanes = lax.broadcasted_iota(jnp.int32, (rows, 128), 1)
    ids[own] = jnp.where(lanes < 64, id_a, id_b)

    def columns(d):
        return pl.ds(pl.multiple_of(other_z[d] * cols, 128), cols)

    wbuf[dp] = weight[:, columns(0)]
    pl.semaphore_wait(barrier, len(peers))
    w_z = {d: push(weight.at[:, columns(d)], wbuf.at[dp], at_z[d]) for d in (2, 1, 3)}

    def spread_weight(zz):
        piece = wbuf.at[zz * QS + q]
        return push(piece, piece, beside_x), push(piece, piece, beside_y), zz

    first = [spread_weight(z)]
    v_z = {}
    for v in range(2):
        for d in (1, 3, 2):
            piece = views.at[v, own, mine]
            v_z[v, d] = push(piece, piece, at_z[d])
    m_z = {d: push(ids.at[own], ids.at[own], at_z[d]) for d in (1, 2, 3)}
    second = []

    def forward_weight(entry):
        via_x, via_y, zz = entry
        via_x.wait_recv()
        piece = wbuf.at[zz * QS + q_x, pl.ds(0, depth // 2)]
        second.append(push(piece, piece, beside_y))
        via_y.wait_recv()
        piece = wbuf.at[zz * QS + q_y, pl.ds(depth // 2, depth // 2)]
        second.append(push(piece, piece, beside_x))

    for d in (1, 3, 2):
        w_z[d].wait_recv()
        first.append(spread_weight(from_z[d]))
        forward_weight(first[-2])
    forward_weight(first[-1])

    steps = [(v, d) for v in range(2) for d in (0, 1, 3, 2)]
    v_s, raw_copies, crossed, stat_copies = {}, {}, {0: [], 1: []}, {}
    many = ZS * rows

    def share_view(v, d):
        if d:
            v_z[v, d].wait_recv()
            piece = views.at[v, block(from_z[d]), mine]
            v_s[v, d] = push(piece, piece, sibling)

    def project(v, d):
        if d:
            v_s[v, d].wait_recv()
        there = block(from_z[d])
        flat = wbuf[...].reshape(width, cols)
        raw[v, q, there] = jnp.dot(views[v, there], flat, preferred_element_type=F32).astype(BF)
        piece = raw.at[v, q, there]
        raw_copies[v, d] = push(piece, piece, beside_x), push(piece, piece, beside_y)

    def forward_raw(v, d):
        start = pl.multiple_of(from_z[d] * rows, rows)
        raw_copies[v, d][0].wait_recv()
        piece = raw.at[v, q_x, pl.ds(start, rows // 2)]
        crossed[v].append(push(piece, piece, beside_y))
        raw_copies[v, d][1].wait_recv()
        piece = raw.at[v, q_y, pl.ds(pl.multiple_of(start + rows // 2, rows // 2), rows // 2)]
        crossed[v].append(push(piece, piece, beside_x))

    def moments(v):
        held = raw[v, q].astype(F32)
        mean = jnp.sum(held, axis=0, keepdims=True) / many
        held = held - mean
        spread = jnp.sum(held * held, axis=0, keepdims=True)
        stat[v, q] = jnp.concatenate([mean, spread, jnp.zeros((6, cols), F32)], axis=0)
        piece = stat.at[v, q]
        stat_copies[v] = [push(piece, piece, peer) for peer in (across, beside_x, beside_y)]

    share_view(*steps[0])
    share_view(*steps[1])
    for copy in second:
        copy.wait_recv()
    for i, step in enumerate(steps):
        project(*step)
        if i + 2 < len(steps):
            share_view(*steps[i + 2])
        if step[1] == 2:
            moments(step[0])
        if i:
            forward_raw(*steps[i - 1])

    inverse = {}

    def gram_part(v):
        for copy in stat_copies[v]:
            copy.wait_recv()
        mean = stat[v, 0, 0:1]
        for i in range(1, QS):
            mean = mean + stat[v, i, 0:1]
        mean = mean / QS
        total = jnp.zeros((1, cols), F32)
        for i in range(QS):
            off = stat[v, i, 0:1] - mean
            total = total + stat[v, i, 1:2] + many * (off * off)
        inv = lax.rsqrt(total / batch + NORM_EPS)
        inverse[v] = inv
        for k, source in enumerate((q, q_x, q_y, QS - 1 - q)):
            if k == QS - 1:
                for copy in crossed[v]:
                    copy.wait_recv()
            norm[v, source] = ((raw[v, source].astype(F32) - mean) * inv).astype(BF)
            gram = contract_last(norm[v, q], norm[v, source]).astype(BF)
            lane = pl.ds(pl.multiple_of(source * many, 128), many)
            for i in range(ZS):
                for core in range(2):
                    start = i * rows + core * (rows // 2)
                    gpart[v, core, i, :, lane] = gram[start : start + rows // 2]
        return push(gpart.at[v, 1 - t], gsib.at[v], sibling)

    def gram_scatter(v, copy):
        copy.wait_recv()
        copies = {}
        for d in (2, 1, 3):
            pair = gpart[v, t, other_z[d]].astype(F32) + gsib[v, other_z[d]].astype(F32)
            gsend[v, d - 1] = pair.astype(BF)
            copies[d] = push(gsend.at[v, d - 1], grecv.at[v, d - 1], at_z[d])
        gsum[v] = gpart[v, t, z].astype(F32) + gsib[v, z].astype(F32)
        return copies

    def gram_sum(v, copies):
        gram = gsum[v]
        for d in (1, 3, 2):
            copies[d].wait_recv()
            gram = gram + grecv[v, d - 1].astype(F32)
        gsum[v] = gram
        gfull[v, z, t] = gram.astype(BF)
        piece = gfull.at[v, z, t]
        return {d: push(piece, piece, at_z[d]) for d in (2, 1, 3)}, [push(piece, piece, sibling)]

    def gram_share(v, along, within):
        for d in (1, 3, 2):
            along[d].wait_recv()
            piece = gfull.at[v, from_z[d], t]
            within.append(push(piece, piece, sibling))

    factor = 2.0 * LAMBDA_OFF / (batch * batch)

    def grad_of(v, slot, extra):
        here, other = norm[v, q].astype(F32), norm[1 - v, q].astype(F32)
        grad = other * (coeff / batch) + factor * jnp.dot(
            gfull[1 - v].reshape(many, batch), norm[v].reshape(batch, cols),
            preferred_element_type=F32,
        )
        parts = [jnp.sum(part, axis=0, keepdims=True) for part in (grad, grad * here)]
        sums[slot, q] = jnp.concatenate(parts + extra + [jnp.zeros((6 - len(extra), cols), F32)], axis=0)
        piece = sums.at[slot, q]
        return grad, [push(piece, piece, peer) for peer in (across, beside_x, beside_y)]

    def summed(slot, copies):
        for copy in copies:
            copy.wait_recv()
        total = sums[slot, 0]
        for i in range(1, QS):
            total = total + sums[slot, i]
        return total

    def norm_back(v, grad, total):
        mean = total / batch
        here = norm[v, q].astype(F32)
        return (inverse[v] * (grad - mean[0:1] - here * mean[1:2])).astype(BF)

    sib_a = gram_part(0)
    forward_raw(*steps[-1])
    z_a = gram_scatter(0, sib_a)
    sib_b = gram_part(1)
    along_a, within_a = gram_sum(0, z_a)
    z_b = gram_scatter(1, sib_b)
    total = jnp.zeros((1, cols), F32)
    for i in range(QS):
        total += jnp.sum(norm[0, i].astype(F32) * norm[1, i].astype(F32), axis=0, keepdims=True)
    diag = total / batch
    coeff = -2.0 * (1.0 - diag) - 2.0 * LAMBDA_OFF * diag
    gram_share(0, along_a, within_a)
    along_b, within_b = gram_sum(1, z_b)
    power = jnp.sum(gsum[0] * gsum[1], keepdims=True)
    small[z] = jnp.concatenate(
        [diag, jnp.broadcast_to(power, (1, cols)), jnp.zeros((6, cols), F32)], axis=0
    )
    small_z = {d: push(small.at[z], small.at[z], at_z[d]) for d in (1, 2, 3)}
    for copy in within_a:
        copy.wait_recv()
    grad, copies = grad_of(1, 0, [])
    for d in (1, 2, 3):
        m_z[d].wait_recv()
    dz_b = norm_back(1, grad, summed(0, copies))
    slabs = wbuf.shape[0] // 4
    chunk = half // 2

    def back(dz, core, c, lane):
        part = wbuf[pl.ds((core * 2 + c) * slabs, slabs)].reshape(chunk, cols)
        group = lax.broadcasted_iota(jnp.int32, (1, chunk), 1) + (core * 2 + c) * chunk
        group = (group // (width // GROUPS)).astype(F32)
        return jnp.where(group != ids[:, lane : lane + 1], contract_last(dz, part), 0.0)

    order = [(1 - t, 0), (1 - t, 1), (t, 0), (t, 1)]
    gram_share(1, along_b, within_b)
    for i, (core, c) in enumerate(order):
        fown[i] = back(dz_b, core, c, 64)
    for copy in within_b:
        copy.wait_recv()
    for d in (1, 2, 3):
        small_z[d].wait_recv()
    power = small[0, 1:2]
    for i in range(1, ZS):
        power = power + small[i, 1:2]
        diag_out[0:1, i * cols : (i + 1) * cols] = small[i, 0:1]
    diag_out[0:1, 0:cols] = small[0, 0:1]
    grad, copies = grad_of(0, 1, [power])
    total = summed(1, copies)
    last[0] = total
    last_copy = push(last.at[0], last.at[1], sibling)
    dz_a = norm_back(0, grad, total)

    f_s, f_z = {}, {}
    for c in range(2):
        fsib_out[c] = (fown[c] + back(dz_a, 1 - t, c, 0)).astype(BF).reshape(ZS, rows, chunk)
        f_s[c] = push(fsib_out.at[c], fsib.at[c], sibling)
    for c in range(2):
        pair = fown[2 + c] + back(dz_a, t, c, 0)
        f_s[c].wait_recv()
        fown[2 + c] = pair + fsib[c].astype(F32).reshape(many, chunk)
        for d in (2, 1, 3):
            fsend[c, d - 1] = fown[2 + c, block(other_z[d])].astype(BF)
            f_z[c, d] = push(fsend.at[c, d - 1], frecv.at[c, d - 1], at_z[d])
    last_copy.wait_recv()
    power = last[0, 2:3, 0:1] + last[1, 2:3, 0:1]
    cross_out[...] = power / (batch * batch) / emb
    for c in range(2):
        result = fown[2 + c, own]
        for d in (1, 3, 2):
            f_z[c, d].wait_recv()
            result = result + frecv[c, d - 1].astype(F32)
        out[:, c * chunk : (c + 1) * chunk] = LOSS_SCALE * result
    for copy in started:
        copy.wait_send()


COPIES = 128


def fused(feats, jitter, mask_ids, proj_weight):
    rows, width = feats.shape
    depth, local = proj_weight.shape
    cols, half, many = local // ZS, width // 2, rows * ZS
    batch = many * QS
    vmem = pl.BlockSpec(memory_space=pltpu.VMEM)
    grad, diag, power = pl.pallas_call(
        functools.partial(fused_kernel, emb=EMB),
        out_shape=(
            jax.ShapeDtypeStruct((rows, half), F32),
            jax.ShapeDtypeStruct((1, local), F32),
            jax.ShapeDtypeStruct((1, 1), F32),
        ),
        in_specs=[vmem] * 4,
        out_specs=(vmem,) * 3,
        scratch_shapes=[
            pltpu.VMEM((2, many, width), BF),
            pltpu.VMEM((many, 128), F32),
            pltpu.VMEM((ZS * QS, depth, cols), BF),
            pltpu.VMEM((2, QS, many, cols), BF),
            pltpu.VMEM((2, QS, many, cols), BF),
            pltpu.VMEM((2, 2, ZS, rows // 2, batch), BF),
            pltpu.VMEM((2, ZS, rows // 2, batch), BF),
            pltpu.VMEM((2, ZS - 1, rows // 2, batch), BF),
            pltpu.VMEM((2, ZS - 1, rows // 2, batch), BF),
            pltpu.VMEM((2, rows // 2, batch), F32),
            pltpu.VMEM((2, ZS, 2, rows // 2, batch), BF),
            pltpu.VMEM((2, QS, 8, cols), F32),
            pltpu.VMEM((ZS, 8, cols), F32),
            pltpu.VMEM((2, QS, 8, cols), F32),
            pltpu.VMEM((2, 8, cols), F32),
            pltpu.VMEM((2, ZS, rows, half // 2), BF),
            pltpu.VMEM((2, ZS, rows, half // 2), BF),
            pltpu.VMEM((4, many, half // 2), F32),
            pltpu.VMEM((2, ZS - 1, rows, half // 2), BF),
            pltpu.VMEM((2, ZS - 1, rows, half // 2), BF),
            pltpu.SemaphoreType.DMA((COPIES,)),
            pltpu.SemaphoreType.DMA((COPIES,)),
        ],
        compiler_params=pltpu.CompilerParams(
            collective_id=0, has_side_effects=True, vmem_limit_bytes=56 * 2**20
        ),
    )(feats, jitter, mask_ids.T, proj_weight)
    return grad, diag.reshape(local), power.reshape(())


def solution(mesh):
    in_specs = (P("dp", None), P("dp", None), P("dp", None), P("dp", "tile"))
    out_specs = (P("dp", "tile"), P("tile"), P())
    planes = mesh.shape["dp"] == ZS * QS and mesh.shape["tile"] == 2
    return jax.shard_map(
        fused if planes else on_device, mesh=mesh, in_specs=in_specs, out_specs=out_specs, check_vma=False
    )
```

```python
import functools
import itertools

import jax
import jax.numpy as jnp
from jax import lax
from jax.experimental import pallas as pl
from jax.experimental.pallas import tpu as pltpu
from jax.sharding import PartitionSpec as P

EMB = 4096
GROUPS = 32


LAMBDA_OFF = 0.0051
NORM_EPS = 1e-05
LOSS_SCALE = 65536.0


def masked_views(feats, jitter, mask_ids):
    width = feats.shape[1]
    group_size = width // GROUPS
    channel_group = lax.broadcasted_iota(jnp.int32, (1, width), 1) // group_size
    keep_a = (channel_group != mask_ids[:, 0:1]).astype(jnp.float32)
    keep_b = (channel_group != mask_ids[:, 1:2]).astype(jnp.float32)
    values = feats.astype(jnp.float32)
    view_a = (values * keep_a).astype(jnp.bfloat16)
    view_b = (values * keep_b + jitter.astype(jnp.float32)).astype(jnp.bfloat16)
    return (view_a, view_b, keep_a, keep_b)


def contract_last(left, right):
    return lax.dot_general(
        left, right, (((1,), (1,)), ((), ())), preferred_element_type=jnp.float32
    )


def on_device(feats, jitter, mask_ids, proj_weight):
    view_a, view_b, keep_a, keep_b = masked_views(feats, jitter, mask_ids)
    rows = feats.shape[0]
    total = rows * lax.axis_size("dp")
    piece = lax.all_gather(proj_weight, "dp", axis=0, tiled=True)
    raw_a = jnp.dot(view_a, piece, preferred_element_type=jnp.float32)
    raw_b = jnp.dot(view_b, piece, preferred_element_type=jnp.float32)
    raw_a = raw_a.astype(jnp.bfloat16)
    raw_b = raw_b.astype(jnp.bfloat16)
    values_a = raw_a.astype(jnp.float32)
    values_b = raw_b.astype(jnp.float32)
    moment_sums = lax.psum(
        (
            jnp.sum(values_a, axis=0),
            jnp.sum(values_a * values_a, axis=0),
            jnp.sum(values_b, axis=0),
            jnp.sum(values_b * values_b, axis=0),
        ),
        "dp",
    )
    mean_a = moment_sums[0] / total
    mean_b = moment_sums[2] / total
    inv_a = lax.rsqrt(moment_sums[1] / total - mean_a * mean_a + NORM_EPS)
    inv_b = lax.rsqrt(moment_sums[3] / total - mean_b * mean_b + NORM_EPS)
    norm_a = ((values_a - mean_a) * inv_a).astype(jnp.bfloat16)
    norm_b = ((values_b - mean_b) * inv_b).astype(jnp.bfloat16)
    outgoing_a, outgoing_b = (norm_a, norm_b)
    gathered_a, gathered_b = (
        lax.all_gather(outgoing_a, "dp", axis=0, tiled=True),
        lax.all_gather(outgoing_b, "dp", axis=0, tiled=True),
    )
    whole_a, whole_b = (gathered_a, gathered_b)
    za = norm_a.astype(jnp.float32)
    zb = norm_b.astype(jnp.float32)
    diag_corr = jnp.sum(whole_a.astype(jnp.float32) * whole_b.astype(jnp.float32), axis=0) / total
    gram_a, gram_b = (
        lax.psum(contract_last(norm_a, whole_a).astype(jnp.bfloat16), "tile").astype(jnp.float32),
        lax.psum(contract_last(norm_b, whole_b).astype(jnp.bfloat16), "tile").astype(jnp.float32),
    )
    trace_part = jnp.sum(gram_a * gram_b)
    gram_bf_a = gram_a.astype(jnp.bfloat16)
    gram_bf_b = gram_b.astype(jnp.bfloat16)
    coeff = -2.0 * (1.0 - diag_corr) - 2.0 * LAMBDA_OFF * diag_corr
    factor = 2.0 * LAMBDA_OFF / (total * total)
    grad_na = zb * coeff / total + factor * jnp.dot(
        gram_bf_b, whole_a, preferred_element_type=jnp.float32
    )
    grad_nb = za * coeff / total + factor * jnp.dot(
        gram_bf_a, whole_b, preferred_element_type=jnp.float32
    )
    sums = lax.psum(
        (
            jnp.sum(grad_na, axis=0),
            jnp.sum(grad_na * za, axis=0),
            jnp.sum(grad_nb, axis=0),
            jnp.sum(grad_nb * zb, axis=0),
            trace_part,
        ),
        "dp",
    )
    dz_a = (inv_a * (grad_na - sums[0] / total - za * (sums[1] / total))).astype(jnp.bfloat16)
    dz_b = (inv_b * (grad_nb - sums[2] / total - zb * (sums[3] / total))).astype(jnp.bfloat16)
    cross_power = sums[4] / (total * total) / EMB
    piece = lax.all_gather(proj_weight, "dp", axis=0, tiled=True)
    combined = keep_a * contract_last(dz_a, piece) + keep_b * contract_last(dz_b, piece)
    feats_grad = LOSS_SCALE * lax.psum_scatter(
        combined.astype(jnp.bfloat16), "tile", scatter_dimension=1, tiled=True
    ).astype(jnp.float32)
    return (feats_grad, diag_corr, cross_power)


ZS = 4
QS = 4
BF, F32 = jnp.bfloat16, jnp.float32


def fused_kernel(
    feats, jitter, mask, weight, out, diag_out, cross_out,
    views, ids, wbuf, raw, norm, gpart, gsib, gsend, grecv, gsum, gfull,
    stat, small, sums, last, fsib_out, fsib, fown, fsend, frecv, send, recv, hop_send, hop_recv, *, emb
):
    dp, t = lax.axis_index("dp"), lax.axis_index("tile")
    rows, width = feats.shape
    depth, local = weight.shape
    cols = local // ZS
    half = width // 2
    batch = rows * ZS * QS
    z, q = dp // QS, lax.rem(dp, QS)
    x, y = lax.rem(q, 2), q // 2
    sibling = (dp, 1 - t)
    beside_x = (dp + 1 - 2 * x, t)
    beside_y = (dp + 2 - 4 * y, t)
    across = (dp + 1 - 2 * x + 2 - 4 * y, t)
    q_x, q_y = q + 1 - 2 * x, q + 2 - 4 * y
    other_z = [lax.rem(z + d, ZS) for d in range(ZS)]
    from_z = [lax.rem(z + ZS - d, ZS) for d in range(ZS)]
    at_z = [(other_z[d] * QS + q, t) for d in range(ZS)]
    numbers = itertools.count()
    started = []

    def push(src, dst, device):
        i = next(numbers)
        copy = pltpu.make_async_remote_copy(
            src_ref=src, dst_ref=dst, send_sem=send.at[i], recv_sem=recv.at[i],
            device_id=device, device_id_type=pl.DeviceIdType.MESH,
        )
        copy.start()
        started.append(copy)
        return copy

    barrier = pltpu.get_barrier_semaphore()
    peers = [sibling, beside_x, beside_y, across] + at_z[1:]
    for peer in peers:
        pl.semaphore_signal(barrier, inc=1, device_id=peer, device_id_type=pl.DeviceIdType.MESH)

    def block(i):
        return pl.ds(pl.multiple_of(i * rows, rows), rows)

    own = block(z)
    mine = pl.ds(pl.multiple_of(t * half, 128), half)

    square = [lax.broadcasted_iota(jnp.int32, (rows, rows), axis) for axis in range(2)]

    def id_column(v):
        row = jnp.broadcast_to(mask[v : v + 1, :].astype(F32), (rows, rows))
        return jnp.sum(jnp.where(square[0] == square[1], row, 0.0), axis=1, keepdims=True)

    id_a, id_b = id_column(0), id_column(1)
    group = lax.broadcasted_iota(jnp.int32, (1, width), 1) // (width // GROUPS)
    group = group.astype(F32)
    values = feats[...].astype(F32)
    views[0, own] = jnp.where(group != id_a, values, 0.0).astype(BF)
    views[1, own] = (jnp.where(group != id_b, values, 0.0) + jitter[...].astype(F32)).astype(BF)
    lanes = lax.broadcasted_iota(jnp.int32, (rows, 128), 1)
    ids[own] = jnp.where(lanes < 64, id_a, id_b)

    def columns(d):
        return pl.ds(pl.multiple_of(other_z[d] * cols, 128), cols)

    wbuf[dp] = weight[:, columns(0)]
    pl.semaphore_wait(barrier, len(peers))
    w_z = {d: push(weight.at[:, columns(d)], wbuf.at[dp], at_z[d]) for d in (2, 1, 3)}

    def spread_weight(zz):
        piece = wbuf.at[zz * QS + q]
        return push(piece, piece, beside_x), push(piece, piece, beside_y), zz

    first = [spread_weight(z)]

    sources = [z, z + 1 - 2 * lax.rem(z, 2), 2 - z // 2, (ZS - 1) * (1 - z // 2)]

    def hop(v, source, up):
        piece = views.at[v, block(source), mine]
        return pltpu.make_async_remote_copy(
            src_ref=piece, dst_ref=piece, send_sem=hop_send.at[v, up, source],
            recv_sem=hop_recv.at[v, source], device_id=(dp + (QS if up else -QS), t),
            device_id_type=pl.DeviceIdType.MESH,
        )

    def hop_on(v, source, act):
        pl.when((source <= z) & (z < ZS - 1))(lambda: act(hop(v, source, 1)))
        pl.when((source >= z) & (z > 0))(lambda: act(hop(v, source, 0)))

    for v in range(2):
        hop_on(v, z, lambda copy: copy.start())
    m_z = {d: push(ids.at[own], ids.at[own], at_z[d]) for d in (1, 2, 3)}
    second = []

    def forward_weight(entry):
        via_x, via_y, zz = entry
        via_x.wait_recv()
        piece = wbuf.at[zz * QS + q_x, pl.ds(0, depth // 2)]
        second.append(push(piece, piece, beside_y))
        via_y.wait_recv()
        piece = wbuf.at[zz * QS + q_y, pl.ds(depth // 2, depth // 2)]
        second.append(push(piece, piece, beside_x))

    steps = [(v, k) for v in range(2) for k in range(ZS)]
    v_s, raw_copies, crossed, stat_copies = {}, {}, {0: [], 1: []}, {}
    many = ZS * rows

    def share_view(v, k):
        if k:
            hop(v, sources[k], 1).wait_recv()
            hop_on(v, sources[k], lambda copy: copy.start())
            piece = views.at[v, block(sources[k]), mine]
            v_s[v, k] = push(piece, piece, sibling)

    def project(v, k):
        if k:
            v_s[v, k].wait_recv()
        there = block(sources[k])
        flat = wbuf[...].reshape(width, cols)
        raw[v, q, there] = jnp.dot(views[v, there], flat, preferred_element_type=F32).astype(BF)
        piece = raw.at[v, q, there]
        raw_copies[v, k] = push(piece, piece, beside_x), push(piece, piece, beside_y)

    def forward_raw(v, k):
        start = pl.multiple_of(sources[k] * rows, rows)
        raw_copies[v, k][0].wait_recv()
        piece = raw.at[v, q_x, pl.ds(start, rows // 2)]
        crossed[v].append(push(piece, piece, beside_y))
        raw_copies[v, k][1].wait_recv()
        piece = raw.at[v, q_y, pl.ds(pl.multiple_of(start + rows // 2, rows // 2), rows // 2)]
        crossed[v].append(push(piece, piece, beside_x))

    def moments(v):
        held = raw[v, q].astype(F32)
        mean = jnp.sum(held, axis=0, keepdims=True) / many
        held = held - mean
        spread = jnp.sum(held * held, axis=0, keepdims=True)
        stat[v, q] = jnp.concatenate([mean, spread, jnp.zeros((6, cols), F32)], axis=0)
        piece = stat.at[v, q]
        stat_copies[v] = [push(piece, piece, peer) for peer in (across, beside_x, beside_y)]

    w_z[1].wait_recv()
    first.append(spread_weight(from_z[1]))
    forward_weight(first[0])
    for d in (3, 2):
        w_z[d].wait_recv()
        first.append(spread_weight(from_z[d]))
    share_view(0, 1)
    forward_weight(first[1])
    share_view(0, 2)
    forward_weight(first[2])
    share_view(0, 3)
    forward_weight(first[3])
    share_view(1, 1)
    for copy in second:
        copy.wait_recv()
    for i, step in enumerate(steps):
        project(*step)
        if step == (0, 1):
            share_view(1, 2)
        if step == (0, 3):
            share_view(1, 3)
        if step[1] == ZS - 1:
            moments(step[0])
        if i:
            forward_raw(*steps[i - 1])

    inverse = {}

    def gram_part(v):
        for copy in stat_copies[v]:
            copy.wait_recv()
        mean = stat[v, 0, 0:1]
        for i in range(1, QS):
            mean = mean + stat[v, i, 0:1]
        mean = mean / QS
        total = jnp.zeros((1, cols), F32)
        for i in range(QS):
            off = stat[v, i, 0:1] - mean
            total = total + stat[v, i, 1:2] + many * (off * off)
        inv = lax.rsqrt(total / batch + NORM_EPS)
        inverse[v] = inv
        for k, source in enumerate((q, q_x, q_y, QS - 1 - q)):
            if k == QS - 1:
                for copy in crossed[v]:
                    copy.wait_recv()
            norm[v, source] = ((raw[v, source].astype(F32) - mean) * inv).astype(BF)
            gram = contract_last(norm[v, q], norm[v, source]).astype(BF)
            lane = pl.ds(pl.multiple_of(source * many, 128), many)
            for i in range(ZS):
                for core in range(2):
                    start = i * rows + core * (rows // 2)
                    gpart[v, core, i, :, lane] = gram[start : start + rows // 2]
        return push(gpart.at[v, 1 - t], gsib.at[v], sibling)

    def gram_scatter(v, copy):
        copy.wait_recv()
        copies = {}
        for d in (2, 1, 3):
            pair = gpart[v, t, other_z[d]].astype(F32) + gsib[v, other_z[d]].astype(F32)
            gsend[v, d - 1] = pair.astype(BF)
            copies[d] = push(gsend.at[v, d - 1], grecv.at[v, d - 1], at_z[d])
        gsum[v] = gpart[v, t, z].astype(F32) + gsib[v, z].astype(F32)
        return copies

    def gram_sum(v, copies):
        gram = gsum[v]
        for d in (1, 3, 2):
            copies[d].wait_recv()
            gram = gram + grecv[v, d - 1].astype(F32)
        gsum[v] = gram
        gfull[v, z, t] = gram.astype(BF)
        piece = gfull.at[v, z, t]
        return {d: push(piece, piece, at_z[d]) for d in (2, 1, 3)}, [push(piece, piece, sibling)]

    def gram_share(v, along, within):
        for d in (1, 3, 2):
            along[d].wait_recv()
            piece = gfull.at[v, from_z[d], t]
            within.append(push(piece, piece, sibling))

    factor = 2.0 * LAMBDA_OFF / (batch * batch)

    def grad_of(v, slot, extra):
        here, other = norm[v, q].astype(F32), norm[1 - v, q].astype(F32)
        grad = other * (coeff / batch) + factor * jnp.dot(
            gfull[1 - v].reshape(many, batch), norm[v].reshape(batch, cols),
            preferred_element_type=F32,
        )
        parts = [jnp.sum(part, axis=0, keepdims=True) for part in (grad, grad * here)]
        sums[slot, q] = jnp.concatenate(parts + extra + [jnp.zeros((6 - len(extra), cols), F32)], axis=0)
        piece = sums.at[slot, q]
        return grad, [push(piece, piece, peer) for peer in (across, beside_x, beside_y)]

    def summed(slot, copies):
        for copy in copies:
            copy.wait_recv()
        total = sums[slot, 0]
        for i in range(1, QS):
            total = total + sums[slot, i]
        return total

    def norm_back(v, grad, total):
        mean = total / batch
        here = norm[v, q].astype(F32)
        return (inverse[v] * (grad - mean[0:1] - here * mean[1:2])).astype(BF)

    sib_a = gram_part(0)
    forward_raw(*steps[-1])
    z_a = gram_scatter(0, sib_a)
    sib_b = gram_part(1)
    along_a, within_a = gram_sum(0, z_a)
    z_b = gram_scatter(1, sib_b)
    total = jnp.zeros((1, cols), F32)
    for i in range(QS):
        total += jnp.sum(norm[0, i].astype(F32) * norm[1, i].astype(F32), axis=0, keepdims=True)
    diag = total / batch
    coeff = -2.0 * (1.0 - diag) - 2.0 * LAMBDA_OFF * diag
    gram_share(0, along_a, within_a)
    along_b, within_b = gram_sum(1, z_b)
    power = jnp.sum(gsum[0] * gsum[1], keepdims=True)
    small[z] = jnp.concatenate(
        [diag, jnp.broadcast_to(power, (1, cols)), jnp.zeros((6, cols), F32)], axis=0
    )
    small_z = {d: push(small.at[z], small.at[z], at_z[d]) for d in (1, 2, 3)}
    for copy in within_a:
        copy.wait_recv()
    grad, copies = grad_of(1, 0, [])
    for d in (1, 2, 3):
        m_z[d].wait_recv()
    dz_b = norm_back(1, grad, summed(0, copies))
    slabs = wbuf.shape[0] // 4
    chunk = half // 2

    def back(dz, core, c, lane):
        part = wbuf[pl.ds((core * 2 + c) * slabs, slabs)].reshape(chunk, cols)
        group = lax.broadcasted_iota(jnp.int32, (1, chunk), 1) + (core * 2 + c) * chunk
        group = (group // (width // GROUPS)).astype(F32)
        return jnp.where(group != ids[:, lane : lane + 1], contract_last(dz, part), 0.0)

    order = [(1 - t, 0), (1 - t, 1), (t, 0), (t, 1)]
    gram_share(1, along_b, within_b)
    for i, (core, c) in enumerate(order):
        fown[i] = back(dz_b, core, c, 64)
    for copy in within_b:
        copy.wait_recv()
    for d in (1, 2, 3):
        small_z[d].wait_recv()
    power = small[0, 1:2]
    for i in range(1, ZS):
        power = power + small[i, 1:2]
        diag_out[0:1, i * cols : (i + 1) * cols] = small[i, 0:1]
    diag_out[0:1, 0:cols] = small[0, 0:1]
    grad, copies = grad_of(0, 1, [power])
    total = summed(1, copies)
    last[0] = total
    last_copy = push(last.at[0], last.at[1], sibling)
    dz_a = norm_back(0, grad, total)

    f_s, f_z = {}, {}
    for c in range(2):
        fsib_out[c] = (fown[c] + back(dz_a, 1 - t, c, 0)).astype(BF).reshape(ZS, rows, chunk)
        f_s[c] = push(fsib_out.at[c], fsib.at[c], sibling)
    for c in range(2):
        pair = fown[2 + c] + back(dz_a, t, c, 0)
        f_s[c].wait_recv()
        fown[2 + c] = pair + fsib[c].astype(F32).reshape(many, chunk)
        for d in (2, 1, 3):
            fsend[c, d - 1] = fown[2 + c, block(other_z[d])].astype(BF)
            f_z[c, d] = push(fsend.at[c, d - 1], frecv.at[c, d - 1], at_z[d])
    last_copy.wait_recv()
    power = last[0, 2:3, 0:1] + last[1, 2:3, 0:1]
    cross_out[...] = power / (batch * batch) / emb
    for c in range(2):
        result = fown[2 + c, own]
        for d in (1, 3, 2):
            f_z[c, d].wait_recv()
            result = result + frecv[c, d - 1].astype(F32)
        out[:, c * chunk : (c + 1) * chunk] = LOSS_SCALE * result
    for copy in started:
        copy.wait_send()
    for v in range(2):
        for source in sources:
            hop_on(v, source, lambda copy: copy.wait_send())


COPIES = 128


def fused(feats, jitter, mask_ids, proj_weight):
    rows, width = feats.shape
    depth, local = proj_weight.shape
    cols, half, many = local // ZS, width // 2, rows * ZS
    batch = many * QS
    vmem = pl.BlockSpec(memory_space=pltpu.VMEM)
    grad, diag, power = pl.pallas_call(
        functools.partial(fused_kernel, emb=EMB),
        out_shape=(
            jax.ShapeDtypeStruct((rows, half), F32),
            jax.ShapeDtypeStruct((1, local), F32),
            jax.ShapeDtypeStruct((1, 1), F32),
        ),
        in_specs=[vmem] * 4,
        out_specs=(vmem,) * 3,
        scratch_shapes=[
            pltpu.VMEM((2, many, width), BF),
            pltpu.VMEM((many, 128), F32),
            pltpu.VMEM((ZS * QS, depth, cols), BF),
            pltpu.VMEM((2, QS, many, cols), BF),
            pltpu.VMEM((2, QS, many, cols), BF),
            pltpu.VMEM((2, 2, ZS, rows // 2, batch), BF),
            pltpu.VMEM((2, ZS, rows // 2, batch), BF),
            pltpu.VMEM((2, ZS - 1, rows // 2, batch), BF),
            pltpu.VMEM((2, ZS - 1, rows // 2, batch), BF),
            pltpu.VMEM((2, rows // 2, batch), F32),
            pltpu.VMEM((2, ZS, 2, rows // 2, batch), BF),
            pltpu.VMEM((2, QS, 8, cols), F32),
            pltpu.VMEM((ZS, 8, cols), F32),
            pltpu.VMEM((2, QS, 8, cols), F32),
            pltpu.VMEM((2, 8, cols), F32),
            pltpu.VMEM((2, ZS, rows, half // 2), BF),
            pltpu.VMEM((2, ZS, rows, half // 2), BF),
            pltpu.VMEM((4, many, half // 2), F32),
            pltpu.VMEM((2, ZS - 1, rows, half // 2), BF),
            pltpu.VMEM((2, ZS - 1, rows, half // 2), BF),
            pltpu.SemaphoreType.DMA((COPIES,)),
            pltpu.SemaphoreType.DMA((COPIES,)),
            pltpu.SemaphoreType.DMA((2, 2, ZS)),
            pltpu.SemaphoreType.DMA((2, ZS)),
        ],
        compiler_params=pltpu.CompilerParams(
            collective_id=0, has_side_effects=True, vmem_limit_bytes=56 * 2**20
        ),
    )(feats, jitter, mask_ids.T, proj_weight)
    return grad, diag.reshape(local), power.reshape(())


def solution(mesh):
    in_specs = (P("dp", None), P("dp", None), P("dp", None), P("dp", "tile"))
    out_specs = (P("dp", "tile"), P("tile"), P())
    planes = mesh.shape["dp"] == ZS * QS and mesh.shape["tile"] == 2
    return jax.shard_map(
        fused if planes else on_device, mesh=mesh, in_specs=in_specs, out_specs=out_specs, check_vma=False
    )
```

```python
import functools
import itertools

import jax
import jax.numpy as jnp
from jax import lax
from jax.experimental import pallas as pl
from jax.experimental.pallas import tpu as pltpu
from jax.sharding import PartitionSpec as P

EMB = 4096
GROUPS = 32


LAMBDA_OFF = 0.0051
NORM_EPS = 1e-05
LOSS_SCALE = 65536.0


def masked_views(feats, jitter, mask_ids):
    width = feats.shape[1]
    group_size = width // GROUPS
    channel_group = lax.broadcasted_iota(jnp.int32, (1, width), 1) // group_size
    keep_a = (channel_group != mask_ids[:, 0:1]).astype(jnp.float32)
    keep_b = (channel_group != mask_ids[:, 1:2]).astype(jnp.float32)
    values = feats.astype(jnp.float32)
    view_a = (values * keep_a).astype(jnp.bfloat16)
    view_b = (values * keep_b + jitter.astype(jnp.float32)).astype(jnp.bfloat16)
    return (view_a, view_b, keep_a, keep_b)


def contract_last(left, right):
    return lax.dot_general(
        left, right, (((1,), (1,)), ((), ())), preferred_element_type=jnp.float32
    )


def on_device(feats, jitter, mask_ids, proj_weight):
    view_a, view_b, keep_a, keep_b = masked_views(feats, jitter, mask_ids)
    rows = feats.shape[0]
    total = rows * lax.axis_size("dp")
    piece = lax.all_gather(proj_weight, "dp", axis=0, tiled=True)
    raw_a = jnp.dot(view_a, piece, preferred_element_type=jnp.float32)
    raw_b = jnp.dot(view_b, piece, preferred_element_type=jnp.float32)
    raw_a = raw_a.astype(jnp.bfloat16)
    raw_b = raw_b.astype(jnp.bfloat16)
    values_a = raw_a.astype(jnp.float32)
    values_b = raw_b.astype(jnp.float32)
    moment_sums = lax.psum(
        (
            jnp.sum(values_a, axis=0),
            jnp.sum(values_a * values_a, axis=0),
            jnp.sum(values_b, axis=0),
            jnp.sum(values_b * values_b, axis=0),
        ),
        "dp",
    )
    mean_a = moment_sums[0] / total
    mean_b = moment_sums[2] / total
    inv_a = lax.rsqrt(moment_sums[1] / total - mean_a * mean_a + NORM_EPS)
    inv_b = lax.rsqrt(moment_sums[3] / total - mean_b * mean_b + NORM_EPS)
    norm_a = ((values_a - mean_a) * inv_a).astype(jnp.bfloat16)
    norm_b = ((values_b - mean_b) * inv_b).astype(jnp.bfloat16)
    outgoing_a, outgoing_b = (norm_a, norm_b)
    gathered_a, gathered_b = (
        lax.all_gather(outgoing_a, "dp", axis=0, tiled=True),
        lax.all_gather(outgoing_b, "dp", axis=0, tiled=True),
    )
    whole_a, whole_b = (gathered_a, gathered_b)
    za = norm_a.astype(jnp.float32)
    zb = norm_b.astype(jnp.float32)
    diag_corr = jnp.sum(whole_a.astype(jnp.float32) * whole_b.astype(jnp.float32), axis=0) / total
    gram_a, gram_b = (
        lax.psum(contract_last(norm_a, whole_a).astype(jnp.bfloat16), "tile").astype(jnp.float32),
        lax.psum(contract_last(norm_b, whole_b).astype(jnp.bfloat16), "tile").astype(jnp.float32),
    )
    trace_part = jnp.sum(gram_a * gram_b)
    gram_bf_a = gram_a.astype(jnp.bfloat16)
    gram_bf_b = gram_b.astype(jnp.bfloat16)
    coeff = -2.0 * (1.0 - diag_corr) - 2.0 * LAMBDA_OFF * diag_corr
    factor = 2.0 * LAMBDA_OFF / (total * total)
    grad_na = zb * coeff / total + factor * jnp.dot(
        gram_bf_b, whole_a, preferred_element_type=jnp.float32
    )
    grad_nb = za * coeff / total + factor * jnp.dot(
        gram_bf_a, whole_b, preferred_element_type=jnp.float32
    )
    sums = lax.psum(
        (
            jnp.sum(grad_na, axis=0),
            jnp.sum(grad_na * za, axis=0),
            jnp.sum(grad_nb, axis=0),
            jnp.sum(grad_nb * zb, axis=0),
            trace_part,
        ),
        "dp",
    )
    dz_a = (inv_a * (grad_na - sums[0] / total - za * (sums[1] / total))).astype(jnp.bfloat16)
    dz_b = (inv_b * (grad_nb - sums[2] / total - zb * (sums[3] / total))).astype(jnp.bfloat16)
    cross_power = sums[4] / (total * total) / EMB
    piece = lax.all_gather(proj_weight, "dp", axis=0, tiled=True)
    combined = keep_a * contract_last(dz_a, piece) + keep_b * contract_last(dz_b, piece)
    feats_grad = LOSS_SCALE * lax.psum_scatter(
        combined.astype(jnp.bfloat16), "tile", scatter_dimension=1, tiled=True
    ).astype(jnp.float32)
    return (feats_grad, diag_corr, cross_power)


ZS = 4
QS = 4
BF, F32 = jnp.bfloat16, jnp.float32


def fused_kernel(
    feats, jitter, mask, weight, out, diag_out, cross_out,
    views, ids, wbuf, raw, norm, gpart, gsib, gsend, grecv, gsum, gfull,
    stat, small, sums, last, fsib_out, fsib, fown, fsend, frecv, send, recv, hop_send, hop_recv, *, emb
):
    dp, t = lax.axis_index("dp"), lax.axis_index("tile")
    rows, width = feats.shape
    depth, local = weight.shape
    cols = local // ZS
    half = width // 2
    batch = rows * ZS * QS
    z, q = dp // QS, lax.rem(dp, QS)
    x, y = lax.rem(q, 2), q // 2
    sibling = (dp, 1 - t)
    beside_x = (dp + 1 - 2 * x, t)
    beside_y = (dp + 2 - 4 * y, t)
    across = (dp + 1 - 2 * x + 2 - 4 * y, t)
    q_x, q_y = q + 1 - 2 * x, q + 2 - 4 * y
    other_z = [lax.rem(z + d, ZS) for d in range(ZS)]
    from_z = [lax.rem(z + ZS - d, ZS) for d in range(ZS)]
    at_z = [(other_z[d] * QS + q, t) for d in range(ZS)]
    numbers = itertools.count()
    started = []

    def push(src, dst, device):
        i = next(numbers)
        copy = pltpu.make_async_remote_copy(
            src_ref=src, dst_ref=dst, send_sem=send.at[i], recv_sem=recv.at[i],
            device_id=device, device_id_type=pl.DeviceIdType.MESH,
        )
        copy.start()
        started.append(copy)
        return copy

    barrier = pltpu.get_barrier_semaphore()
    peers = [sibling, beside_x, beside_y, across] + at_z[1:]
    for peer in peers:
        pl.semaphore_signal(barrier, inc=1, device_id=peer, device_id_type=pl.DeviceIdType.MESH)

    def block(i):
        return pl.ds(pl.multiple_of(i * rows, rows), rows)

    own = block(z)
    mine = pl.ds(pl.multiple_of(t * half, 128), half)

    square = [lax.broadcasted_iota(jnp.int32, (rows, rows), axis) for axis in range(2)]

    def id_column(v):
        row = jnp.broadcast_to(mask[v : v + 1, :].astype(F32), (rows, rows))
        return jnp.sum(jnp.where(square[0] == square[1], row, 0.0), axis=1, keepdims=True)

    id_a, id_b = id_column(0), id_column(1)
    group = lax.broadcasted_iota(jnp.int32, (1, width), 1) // (width // GROUPS)
    group = group.astype(F32)
    values = feats[...].astype(F32)
    views[0, own] = jnp.where(group != id_a, values, 0.0).astype(BF)
    views[1, own] = (jnp.where(group != id_b, values, 0.0) + jitter[...].astype(F32)).astype(BF)
    lanes = lax.broadcasted_iota(jnp.int32, (rows, 128), 1)
    ids[own] = jnp.where(lanes < 64, id_a, id_b)

    def columns(d):
        return pl.ds(pl.multiple_of(other_z[d] * cols, 128), cols)

    wbuf[dp] = weight[:, columns(0)]
    pl.semaphore_wait(barrier, len(peers))
    w_z = {d: push(weight.at[:, columns(d)], wbuf.at[dp], at_z[d]) for d in (2, 1, 3)}

    def spread_weight(zz):
        piece = wbuf.at[zz * QS + q]
        return push(piece, piece, beside_x), push(piece, piece, beside_y), zz

    first = [spread_weight(z)]

    sources = [z, z + 1 - 2 * lax.rem(z, 2), 2 - z // 2, (ZS - 1) * (1 - z // 2)]

    def hop(v, source, up):
        piece = views.at[v, block(source), mine]
        return pltpu.make_async_remote_copy(
            src_ref=piece, dst_ref=piece, send_sem=hop_send.at[v, up, source],
            recv_sem=hop_recv.at[v, source], device_id=(dp + (QS if up else -QS), t),
            device_id_type=pl.DeviceIdType.MESH,
        )

    def hop_on(v, source, act):
        pl.when((source <= z) & (z < ZS - 1))(lambda: act(hop(v, source, 1)))
        pl.when((source >= z) & (z > 0))(lambda: act(hop(v, source, 0)))

    second = []

    def forward_weight(entry):
        via_x, via_y, zz = entry
        via_x.wait_recv()
        piece = wbuf.at[zz * QS + q_x, pl.ds(0, depth // 2)]
        second.append(push(piece, piece, beside_y))
        via_y.wait_recv()
        piece = wbuf.at[zz * QS + q_y, pl.ds(depth // 2, depth // 2)]
        second.append(push(piece, piece, beside_x))

    v_s, raw_copies, crossed, stat_copies = {}, {}, {0: [], 1: []}, {}
    many = ZS * rows

    def share_view(v, k):
        if k:
            hop(v, sources[k], 1).wait_recv()
            hop_on(v, sources[k], lambda copy: copy.start())
            piece = views.at[v, block(sources[k]), mine]
            v_s[v, k] = push(piece, piece, sibling)

    def project(v):
        for k in range(1, ZS):
            v_s[v, k].wait_recv()
        flat = wbuf[...].reshape(width, cols)
        raw[v, q] = jnp.dot(views[v], flat, preferred_element_type=F32).astype(BF)
        for k in range(2):
            piece = raw.at[v, q, pl.ds(k * many // 2, many // 2)]
            raw_copies[v, k] = push(piece, piece, beside_x), push(piece, piece, beside_y)

    def forward_raw(v, k):
        start = k * many // 2
        raw_copies[v, k][0].wait_recv()
        piece = raw.at[v, q_x, pl.ds(start, many // 4)]
        crossed[v].append(push(piece, piece, beside_y))
        raw_copies[v, k][1].wait_recv()
        piece = raw.at[v, q_y, pl.ds(start + many // 4, many // 4)]
        crossed[v].append(push(piece, piece, beside_x))

    def moments(v):
        held = raw[v, q].astype(F32)
        mean = jnp.sum(held, axis=0, keepdims=True) / many
        held = held - mean
        spread = jnp.sum(held * held, axis=0, keepdims=True)
        stat[v, q] = jnp.concatenate([mean, spread, jnp.zeros((6, cols), F32)], axis=0)
        piece = stat.at[v, q]
        stat_copies[v] = [push(piece, piece, peer) for peer in (across, beside_x, beside_y)]

    for d in (1, 3, 2):
        w_z[d].wait_recv()
        first.append(spread_weight(from_z[d]))
        if d == 1:
            forward_weight(first[0])
    hop_on(0, z, lambda copy: copy.start())
    forward_weight(first[1])
    share_view(0, 1)
    hop_on(1, z, lambda copy: copy.start())
    forward_weight(first[2])
    share_view(0, 2)
    forward_weight(first[3])
    share_view(0, 3)
    share_view(1, 1)
    for copy in second:
        copy.wait_recv()
    project(0)
    moments(0)
    share_view(1, 2)
    forward_raw(0, 0)
    share_view(1, 3)
    forward_raw(0, 1)
    m_z = {d: push(ids.at[own], ids.at[own], at_z[d]) for d in (1, 2, 3)}
    project(1)
    moments(1)

    inverse = {}

    def gram_part(v):
        for copy in stat_copies[v]:
            copy.wait_recv()
        mean = stat[v, 0, 0:1]
        for i in range(1, QS):
            mean = mean + stat[v, i, 0:1]
        mean = mean / QS
        total = jnp.zeros((1, cols), F32)
        for i in range(QS):
            off = stat[v, i, 0:1] - mean
            total = total + stat[v, i, 1:2] + many * (off * off)
        inv = lax.rsqrt(total / batch + NORM_EPS)
        inverse[v] = inv
        for k, source in enumerate((q, q_x, q_y, QS - 1 - q)):
            if k == QS - 1:
                for copy in crossed[v]:
                    copy.wait_recv()
            norm[v, source] = ((raw[v, source].astype(F32) - mean) * inv).astype(BF)
            gram = contract_last(norm[v, q], norm[v, source]).astype(BF)
            lane = pl.ds(pl.multiple_of(source * many, 128), many)
            for i in range(ZS):
                for core in range(2):
                    start = i * rows + core * (rows // 2)
                    gpart[v, core, i, :, lane] = gram[start : start + rows // 2]
        return push(gpart.at[v, 1 - t], gsib.at[v], sibling)

    def gram_scatter(v, copy):
        copy.wait_recv()
        copies = {}
        for d in (2, 1, 3):
            pair = gpart[v, t, other_z[d]].astype(F32) + gsib[v, other_z[d]].astype(F32)
            gsend[v, d - 1] = pair.astype(BF)
            copies[d] = push(gsend.at[v, d - 1], grecv.at[v, d - 1], at_z[d])
        gsum[v] = gpart[v, t, z].astype(F32) + gsib[v, z].astype(F32)
        return copies

    def gram_sum(v, copies):
        gram = gsum[v]
        for d in (1, 3, 2):
            copies[d].wait_recv()
            gram = gram + grecv[v, d - 1].astype(F32)
        gsum[v] = gram
        gfull[v, z, t] = gram.astype(BF)
        piece = gfull.at[v, z, t]
        return {d: push(piece, piece, at_z[d]) for d in (2, 1, 3)}, [push(piece, piece, sibling)]

    def gram_share(v, along, within):
        for d in (1, 3, 2):
            along[d].wait_recv()
            piece = gfull.at[v, from_z[d], t]
            within.append(push(piece, piece, sibling))

    factor = 2.0 * LAMBDA_OFF / (batch * batch)

    def grad_of(v, slot, extra):
        here, other = norm[v, q].astype(F32), norm[1 - v, q].astype(F32)
        grad = other * (coeff / batch) + factor * jnp.dot(
            gfull[1 - v].reshape(many, batch), norm[v].reshape(batch, cols),
            preferred_element_type=F32,
        )
        parts = [jnp.sum(part, axis=0, keepdims=True) for part in (grad, grad * here)]
        sums[slot, q] = jnp.concatenate(parts + extra + [jnp.zeros((6 - len(extra), cols), F32)], axis=0)
        piece = sums.at[slot, q]
        return grad, [push(piece, piece, peer) for peer in (across, beside_x, beside_y)]

    def summed(slot, copies):
        for copy in copies:
            copy.wait_recv()
        total = sums[slot, 0]
        for i in range(1, QS):
            total = total + sums[slot, i]
        return total

    def norm_back(v, grad, total):
        mean = total / batch
        here = norm[v, q].astype(F32)
        return (inverse[v] * (grad - mean[0:1] - here * mean[1:2])).astype(BF)

    sib_a = gram_part(0)
    forward_raw(1, 0)
    z_a = gram_scatter(0, sib_a)
    forward_raw(1, 1)
    sib_b = gram_part(1)
    along_a, within_a = gram_sum(0, z_a)
    z_b = gram_scatter(1, sib_b)
    total = jnp.zeros((1, cols), F32)
    for i in range(QS):
        total += jnp.sum(norm[0, i].astype(F32) * norm[1, i].astype(F32), axis=0, keepdims=True)
    diag = total / batch
    coeff = -2.0 * (1.0 - diag) - 2.0 * LAMBDA_OFF * diag
    gram_share(0, along_a, within_a)
    along_b, within_b = gram_sum(1, z_b)
    power = jnp.sum(gsum[0] * gsum[1], keepdims=True)
    small[z] = jnp.concatenate(
        [diag, jnp.broadcast_to(power, (1, cols)), jnp.zeros((6, cols), F32)], axis=0
    )
    small_z = {d: push(small.at[z], small.at[z], at_z[d]) for d in (1, 2, 3)}
    for copy in within_a:
        copy.wait_recv()
    grad, copies = grad_of(1, 0, [])
    for d in (1, 2, 3):
        m_z[d].wait_recv()
    dz_b = norm_back(1, grad, summed(0, copies))
    slabs = wbuf.shape[0] // 4
    chunk = half // 2

    def back(dz, core, c, lane):
        part = wbuf[pl.ds((core * 2 + c) * slabs, slabs)].reshape(chunk, cols)
        group = lax.broadcasted_iota(jnp.int32, (1, chunk), 1) + (core * 2 + c) * chunk
        group = (group // (width // GROUPS)).astype(F32)
        return jnp.where(group != ids[:, lane : lane + 1], contract_last(dz, part), 0.0)

    order = [(1 - t, 0), (1 - t, 1), (t, 0), (t, 1)]
    gram_share(1, along_b, within_b)
    for i, (core, c) in enumerate(order):
        fown[i] = back(dz_b, core, c, 64)
    for copy in within_b:
        copy.wait_recv()
    for d in (1, 2, 3):
        small_z[d].wait_recv()
    power = small[0, 1:2]
    for i in range(1, ZS):
        power = power + small[i, 1:2]
        diag_out[0:1, i * cols : (i + 1) * cols] = small[i, 0:1]
    diag_out[0:1, 0:cols] = small[0, 0:1]
    grad, copies = grad_of(0, 1, [power])
    total = summed(1, copies)
    last[0] = total
    last_copy = push(last.at[0], last.at[1], sibling)
    dz_a = norm_back(0, grad, total)

    f_s, f_z = {}, {}
    for c in range(2):
        fsib_out[c] = (fown[c] + back(dz_a, 1 - t, c, 0)).astype(BF).reshape(ZS, rows, chunk)
        f_s[c] = push(fsib_out.at[c], fsib.at[c], sibling)
    for c in range(2):
        pair = fown[2 + c] + back(dz_a, t, c, 0)
        f_s[c].wait_recv()
        fown[2 + c] = pair + fsib[c].astype(F32).reshape(many, chunk)
        for d in (2, 1, 3):
            fsend[c, d - 1] = fown[2 + c, block(other_z[d])].astype(BF)
            f_z[c, d] = push(fsend.at[c, d - 1], frecv.at[c, d - 1], at_z[d])
    last_copy.wait_recv()
    power = last[0, 2:3, 0:1] + last[1, 2:3, 0:1]
    cross_out[...] = power / (batch * batch) / emb
    for c in range(2):
        result = fown[2 + c, own]
        for d in (1, 3, 2):
            f_z[c, d].wait_recv()
            result = result + frecv[c, d - 1].astype(F32)
        out[:, c * chunk : (c + 1) * chunk] = LOSS_SCALE * result
    for copy in started:
        copy.wait_send()
    for v in range(2):
        for source in sources:
            hop_on(v, source, lambda copy: copy.wait_send())


COPIES = 128


def fused(feats, jitter, mask_ids, proj_weight):
    rows, width = feats.shape
    depth, local = proj_weight.shape
    cols, half, many = local // ZS, width // 2, rows * ZS
    batch = many * QS
    vmem = pl.BlockSpec(memory_space=pltpu.VMEM)
    grad, diag, power = pl.pallas_call(
        functools.partial(fused_kernel, emb=EMB),
        out_shape=(
            jax.ShapeDtypeStruct((rows, half), F32),
            jax.ShapeDtypeStruct((1, local), F32),
            jax.ShapeDtypeStruct((1, 1), F32),
        ),
        in_specs=[vmem] * 4,
        out_specs=(vmem,) * 3,
        scratch_shapes=[
            pltpu.VMEM((2, many, width), BF),
            pltpu.VMEM((many, 128), F32),
            pltpu.VMEM((ZS * QS, depth, cols), BF),
            pltpu.VMEM((2, QS, many, cols), BF),
            pltpu.VMEM((2, QS, many, cols), BF),
            pltpu.VMEM((2, 2, ZS, rows // 2, batch), BF),
            pltpu.VMEM((2, ZS, rows // 2, batch), BF),
            pltpu.VMEM((2, ZS - 1, rows // 2, batch), BF),
            pltpu.VMEM((2, ZS - 1, rows // 2, batch), BF),
            pltpu.VMEM((2, rows // 2, batch), F32),
            pltpu.VMEM((2, ZS, 2, rows // 2, batch), BF),
            pltpu.VMEM((2, QS, 8, cols), F32),
            pltpu.VMEM((ZS, 8, cols), F32),
            pltpu.VMEM((2, QS, 8, cols), F32),
            pltpu.VMEM((2, 8, cols), F32),
            pltpu.VMEM((2, ZS, rows, half // 2), BF),
            pltpu.VMEM((2, ZS, rows, half // 2), BF),
            pltpu.VMEM((4, many, half // 2), F32),
            pltpu.VMEM((2, ZS - 1, rows, half // 2), BF),
            pltpu.VMEM((2, ZS - 1, rows, half // 2), BF),
            pltpu.SemaphoreType.DMA((COPIES,)),
            pltpu.SemaphoreType.DMA((COPIES,)),
            pltpu.SemaphoreType.DMA((2, 2, ZS)),
            pltpu.SemaphoreType.DMA((2, ZS)),
        ],
        compiler_params=pltpu.CompilerParams(
            collective_id=0, has_side_effects=True, vmem_limit_bytes=56 * 2**20
        ),
    )(feats, jitter, mask_ids.T, proj_weight)
    return grad, diag.reshape(local), power.reshape(())


def solution(mesh):
    in_specs = (P("dp", None), P("dp", None), P("dp", None), P("dp", "tile"))
    out_specs = (P("dp", "tile"), P("tile"), P())
    planes = mesh.shape["dp"] == ZS * QS and mesh.shape["tile"] == 2
    return jax.shard_map(
        fused if planes else on_device, mesh=mesh, in_specs=in_specs, out_specs=out_specs, check_vma=False
    )
```

```python
import functools
import itertools

import jax
import jax.numpy as jnp
from jax import lax
from jax.experimental import pallas as pl
from jax.experimental.pallas import tpu as pltpu
from jax.sharding import PartitionSpec as P

EMB = 4096
GROUPS = 32


LAMBDA_OFF = 0.0051
NORM_EPS = 1e-05
LOSS_SCALE = 65536.0


def masked_views(feats, jitter, mask_ids):
    width = feats.shape[1]
    group_size = width // GROUPS
    channel_group = lax.broadcasted_iota(jnp.int32, (1, width), 1) // group_size
    keep_a = (channel_group != mask_ids[:, 0:1]).astype(jnp.float32)
    keep_b = (channel_group != mask_ids[:, 1:2]).astype(jnp.float32)
    values = feats.astype(jnp.float32)
    view_a = (values * keep_a).astype(jnp.bfloat16)
    view_b = (values * keep_b + jitter.astype(jnp.float32)).astype(jnp.bfloat16)
    return (view_a, view_b, keep_a, keep_b)


def contract_last(left, right):
    return lax.dot_general(
        left, right, (((1,), (1,)), ((), ())), preferred_element_type=jnp.float32
    )


def on_device(feats, jitter, mask_ids, proj_weight):
    view_a, view_b, keep_a, keep_b = masked_views(feats, jitter, mask_ids)
    rows = feats.shape[0]
    total = rows * lax.axis_size("dp")
    piece = lax.all_gather(proj_weight, "dp", axis=0, tiled=True)
    raw_a = jnp.dot(view_a, piece, preferred_element_type=jnp.float32)
    raw_b = jnp.dot(view_b, piece, preferred_element_type=jnp.float32)
    raw_a = raw_a.astype(jnp.bfloat16)
    raw_b = raw_b.astype(jnp.bfloat16)
    values_a = raw_a.astype(jnp.float32)
    values_b = raw_b.astype(jnp.float32)
    moment_sums = lax.psum(
        (
            jnp.sum(values_a, axis=0),
            jnp.sum(values_a * values_a, axis=0),
            jnp.sum(values_b, axis=0),
            jnp.sum(values_b * values_b, axis=0),
        ),
        "dp",
    )
    mean_a = moment_sums[0] / total
    mean_b = moment_sums[2] / total
    inv_a = lax.rsqrt(moment_sums[1] / total - mean_a * mean_a + NORM_EPS)
    inv_b = lax.rsqrt(moment_sums[3] / total - mean_b * mean_b + NORM_EPS)
    norm_a = ((values_a - mean_a) * inv_a).astype(jnp.bfloat16)
    norm_b = ((values_b - mean_b) * inv_b).astype(jnp.bfloat16)
    outgoing_a, outgoing_b = (norm_a, norm_b)
    gathered_a, gathered_b = (
        lax.all_gather(outgoing_a, "dp", axis=0, tiled=True),
        lax.all_gather(outgoing_b, "dp", axis=0, tiled=True),
    )
    whole_a, whole_b = (gathered_a, gathered_b)
    za = norm_a.astype(jnp.float32)
    zb = norm_b.astype(jnp.float32)
    diag_corr = jnp.sum(whole_a.astype(jnp.float32) * whole_b.astype(jnp.float32), axis=0) / total
    gram_a, gram_b = (
        lax.psum(contract_last(norm_a, whole_a).astype(jnp.bfloat16), "tile").astype(jnp.float32),
        lax.psum(contract_last(norm_b, whole_b).astype(jnp.bfloat16), "tile").astype(jnp.float32),
    )
    trace_part = jnp.sum(gram_a * gram_b)
    gram_bf_a = gram_a.astype(jnp.bfloat16)
    gram_bf_b = gram_b.astype(jnp.bfloat16)
    coeff = -2.0 * (1.0 - diag_corr) - 2.0 * LAMBDA_OFF * diag_corr
    factor = 2.0 * LAMBDA_OFF / (total * total)
    grad_na = zb * coeff / total + factor * jnp.dot(
        gram_bf_b, whole_a, preferred_element_type=jnp.float32
    )
    grad_nb = za * coeff / total + factor * jnp.dot(
        gram_bf_a, whole_b, preferred_element_type=jnp.float32
    )
    sums = lax.psum(
        (
            jnp.sum(grad_na, axis=0),
            jnp.sum(grad_na * za, axis=0),
            jnp.sum(grad_nb, axis=0),
            jnp.sum(grad_nb * zb, axis=0),
            trace_part,
        ),
        "dp",
    )
    dz_a = (inv_a * (grad_na - sums[0] / total - za * (sums[1] / total))).astype(jnp.bfloat16)
    dz_b = (inv_b * (grad_nb - sums[2] / total - zb * (sums[3] / total))).astype(jnp.bfloat16)
    cross_power = sums[4] / (total * total) / EMB
    piece = lax.all_gather(proj_weight, "dp", axis=0, tiled=True)
    combined = keep_a * contract_last(dz_a, piece) + keep_b * contract_last(dz_b, piece)
    feats_grad = LOSS_SCALE * lax.psum_scatter(
        combined.astype(jnp.bfloat16), "tile", scatter_dimension=1, tiled=True
    ).astype(jnp.float32)
    return (feats_grad, diag_corr, cross_power)


ZS = 4
QS = 4
BF, F32 = jnp.bfloat16, jnp.float32


def fused_kernel(
    feats, jitter, mask, weight, out, diag_out, cross_out,
    views, ids, wbuf, raw, norm, gpart, gsib, gsend, grecv, gsum, gfull,
    stat, small, sums, last, fsib_out, fsib, fown, fsend, frecv, send, recv, hop_send, hop_recv, *, emb
):
    dp, t = lax.axis_index("dp"), lax.axis_index("tile")
    rows, width = feats.shape
    depth, local = weight.shape
    cols = local // ZS
    half = width // 2
    batch = rows * ZS * QS
    z, q = dp // QS, lax.rem(dp, QS)
    x, y = lax.rem(q, 2), q // 2
    sibling = (dp, 1 - t)
    beside_x = (dp + 1 - 2 * x, t)
    beside_y = (dp + 2 - 4 * y, t)
    across = (dp + 1 - 2 * x + 2 - 4 * y, t)
    q_x, q_y = q + 1 - 2 * x, q + 2 - 4 * y
    other_z = [lax.rem(z + d, ZS) for d in range(ZS)]
    from_z = [lax.rem(z + ZS - d, ZS) for d in range(ZS)]
    at_z = [(other_z[d] * QS + q, t) for d in range(ZS)]
    numbers = itertools.count()
    started = []

    def push(src, dst, device):
        i = next(numbers)
        copy = pltpu.make_async_remote_copy(
            src_ref=src, dst_ref=dst, send_sem=send.at[i], recv_sem=recv.at[i],
            device_id=device, device_id_type=pl.DeviceIdType.MESH,
        )
        copy.start()
        started.append(copy)
        return copy

    barrier = pltpu.get_barrier_semaphore()
    peers = [sibling, beside_x, beside_y, across] + at_z[1:]
    for peer in peers:
        pl.semaphore_signal(barrier, inc=1, device_id=peer, device_id_type=pl.DeviceIdType.MESH)

    def block(i):
        return pl.ds(pl.multiple_of(i * rows, rows), rows)

    own = block(z)
    mine = pl.ds(pl.multiple_of(t * half, 128), half)

    def columns(d):
        return pl.ds(pl.multiple_of(other_z[d] * cols, 128), cols)

    wbuf[dp] = weight[:, columns(0)]
    pl.semaphore_wait(barrier, len(peers))
    w_z = {d: push(weight.at[:, columns(d)], wbuf.at[dp], at_z[d]) for d in (2, 1, 3)}

    def spread_weight(zz):
        piece = wbuf.at[zz * QS + q]
        return push(piece, piece, beside_x), push(piece, piece, beside_y), zz

    first = [spread_weight(z)]

    square = [lax.broadcasted_iota(jnp.int32, (rows, rows), axis) for axis in range(2)]

    def id_column(v):
        row = jnp.broadcast_to(mask[v : v + 1, :].astype(F32), (rows, rows))
        return jnp.sum(jnp.where(square[0] == square[1], row, 0.0), axis=1, keepdims=True)

    id_a, id_b = id_column(0), id_column(1)
    group = lax.broadcasted_iota(jnp.int32, (1, width), 1) // (width // GROUPS)
    group = group.astype(F32)
    values = feats[...].astype(F32)
    views[0, own] = jnp.where(group != id_a, values, 0.0).astype(BF)
    views[1, own] = (jnp.where(group != id_b, values, 0.0) + jitter[...].astype(F32)).astype(BF)
    lanes = lax.broadcasted_iota(jnp.int32, (rows, 128), 1)
    ids[own] = jnp.where(lanes < 64, id_a, id_b)


    sources = [z, z + 1 - 2 * lax.rem(z, 2), 2 - z // 2, (ZS - 1) * (1 - z // 2)]

    def hop(v, source, up):
        piece = views.at[v, block(source), mine]
        return pltpu.make_async_remote_copy(
            src_ref=piece, dst_ref=piece, send_sem=hop_send.at[v, up, source],
            recv_sem=hop_recv.at[v, source], device_id=(dp + (QS if up else -QS), t),
            device_id_type=pl.DeviceIdType.MESH,
        )

    def hop_on(v, source, act):
        pl.when((source <= z) & (z < ZS - 1))(lambda: act(hop(v, source, 1)))
        pl.when((source >= z) & (z > 0))(lambda: act(hop(v, source, 0)))

    second = []

    def forward_weight(entry):
        via_x, via_y, zz = entry
        via_x.wait_recv()
        piece = wbuf.at[zz * QS + q_x, pl.ds(0, depth // 2)]
        second.append(push(piece, piece, beside_y))
        via_y.wait_recv()
        piece = wbuf.at[zz * QS + q_y, pl.ds(depth // 2, depth // 2)]
        second.append(push(piece, piece, beside_x))

    v_s, raw_copies, crossed, stat_copies = {}, {}, {0: [], 1: []}, {}
    many = ZS * rows

    def share_view(v, k):
        if k:
            hop(v, sources[k], 1).wait_recv()
            hop_on(v, sources[k], lambda copy: copy.start())
            piece = views.at[v, block(sources[k]), mine]
            v_s[v, k] = push(piece, piece, sibling)

    def project(v):
        for k in range(1, ZS):
            v_s[v, k].wait_recv()
        flat = wbuf[...].reshape(width, cols)
        raw[v, q] = jnp.dot(views[v], flat, preferred_element_type=F32).astype(BF)
        for k in range(2):
            piece = raw.at[v, q, pl.ds(k * many // 2, many // 2)]
            raw_copies[v, k] = push(piece, piece, beside_x), push(piece, piece, beside_y)

    def forward_raw(v, k):
        start = k * many // 2
        raw_copies[v, k][0].wait_recv()
        piece = raw.at[v, q_x, pl.ds(start, many // 4)]
        crossed[v].append(push(piece, piece, beside_y))
        raw_copies[v, k][1].wait_recv()
        piece = raw.at[v, q_y, pl.ds(start + many // 4, many // 4)]
        crossed[v].append(push(piece, piece, beside_x))

    def moments(v):
        held = raw[v, q].astype(F32)
        mean = jnp.sum(held, axis=0, keepdims=True) / many
        held = held - mean
        spread = jnp.sum(held * held, axis=0, keepdims=True)
        stat[v, q] = jnp.concatenate([mean, spread, jnp.zeros((6, cols), F32)], axis=0)
        piece = stat.at[v, q]
        stat_copies[v] = [push(piece, piece, peer) for peer in (across, beside_x, beside_y)]

    for d in (1, 3, 2):
        w_z[d].wait_recv()
        first.append(spread_weight(from_z[d]))
        if d == 1:
            forward_weight(first[0])
    hop_on(0, z, lambda copy: copy.start())
    forward_weight(first[1])
    share_view(0, 1)
    hop_on(1, z, lambda copy: copy.start())
    forward_weight(first[2])
    share_view(0, 2)
    forward_weight(first[3])
    share_view(0, 3)
    share_view(1, 1)
    for copy in second:
        copy.wait_recv()
    project(0)
    moments(0)
    share_view(1, 2)
    forward_raw(0, 0)
    share_view(1, 3)
    forward_raw(0, 1)
    m_z = {d: push(ids.at[own], ids.at[own], at_z[d]) for d in (1, 2, 3)}
    project(1)
    moments(1)

    inverse = {}

    def gram_part(v):
        for copy in stat_copies[v]:
            copy.wait_recv()
        mean = stat[v, 0, 0:1]
        for i in range(1, QS):
            mean = mean + stat[v, i, 0:1]
        mean = mean / QS
        total = jnp.zeros((1, cols), F32)
        for i in range(QS):
            off = stat[v, i, 0:1] - mean
            total = total + stat[v, i, 1:2] + many * (off * off)
        inv = lax.rsqrt(total / batch + NORM_EPS)
        inverse[v] = inv
        for k, source in enumerate((q, q_x, q_y, QS - 1 - q)):
            if k == QS - 1:
                for copy in crossed[v]:
                    copy.wait_recv()
            norm[v, source] = ((raw[v, source].astype(F32) - mean) * inv).astype(BF)
            gram = contract_last(norm[v, q], norm[v, source]).astype(BF)
            lane = pl.ds(pl.multiple_of(source * many, 128), many)
            for i in range(ZS):
                for core in range(2):
                    start = i * rows + core * (rows // 2)
                    gpart[v, core, i, :, lane] = gram[start : start + rows // 2]
        return push(gpart.at[v, 1 - t], gsib.at[v], sibling)

    def gram_scatter(v, copy):
        copy.wait_recv()
        copies = {}
        for d in (2, 1, 3):
            pair = gpart[v, t, other_z[d]].astype(F32) + gsib[v, other_z[d]].astype(F32)
            gsend[v, d - 1] = pair.astype(BF)
            copies[d] = push(gsend.at[v, d - 1], grecv.at[v, d - 1], at_z[d])
        gsum[v] = gpart[v, t, z].astype(F32) + gsib[v, z].astype(F32)
        return copies

    def gram_sum(v, copies):
        gram = gsum[v]
        for d in (1, 3, 2):
            copies[d].wait_recv()
            gram = gram + grecv[v, d - 1].astype(F32)
        gsum[v] = gram
        gfull[v, z, t] = gram.astype(BF)
        piece = gfull.at[v, z, t]
        return {d: push(piece, piece, at_z[d]) for d in (2, 1, 3)}, [push(piece, piece, sibling)]

    def gram_share(v, along, within):
        for d in (1, 3, 2):
            along[d].wait_recv()
            piece = gfull.at[v, from_z[d], t]
            within.append(push(piece, piece, sibling))

    factor = 2.0 * LAMBDA_OFF / (batch * batch)

    def grad_of(v, slot, extra):
        here, other = norm[v, q].astype(F32), norm[1 - v, q].astype(F32)
        grad = other * (coeff / batch) + factor * jnp.dot(
            gfull[1 - v].reshape(many, batch), norm[v].reshape(batch, cols),
            preferred_element_type=F32,
        )
        parts = [jnp.sum(part, axis=0, keepdims=True) for part in (grad, grad * here)]
        sums[slot, q] = jnp.concatenate(parts + extra + [jnp.zeros((6 - len(extra), cols), F32)], axis=0)
        piece = sums.at[slot, q]
        return grad, [push(piece, piece, peer) for peer in (across, beside_x, beside_y)]

    def summed(slot, copies):
        for copy in copies:
            copy.wait_recv()
        total = sums[slot, 0]
        for i in range(1, QS):
            total = total + sums[slot, i]
        return total

    def norm_back(v, grad, total):
        mean = total / batch
        here = norm[v, q].astype(F32)
        return (inverse[v] * (grad - mean[0:1] - here * mean[1:2])).astype(BF)

    sib_a = gram_part(0)
    forward_raw(1, 0)
    z_a = gram_scatter(0, sib_a)
    forward_raw(1, 1)
    sib_b = gram_part(1)
    along_a, within_a = gram_sum(0, z_a)
    z_b = gram_scatter(1, sib_b)
    total = jnp.zeros((1, cols), F32)
    for i in range(QS):
        total += jnp.sum(norm[0, i].astype(F32) * norm[1, i].astype(F32), axis=0, keepdims=True)
    diag = total / batch
    coeff = -2.0 * (1.0 - diag) - 2.0 * LAMBDA_OFF * diag
    gram_share(0, along_a, within_a)
    along_b, within_b = gram_sum(1, z_b)
    power = jnp.sum(gsum[0] * gsum[1], keepdims=True)
    small[z] = jnp.concatenate(
        [diag, jnp.broadcast_to(power, (1, cols)), jnp.zeros((6, cols), F32)], axis=0
    )
    small_z = {d: push(small.at[z], small.at[z], at_z[d]) for d in (1, 2, 3)}
    for copy in within_a:
        copy.wait_recv()
    grad, copies = grad_of(1, 0, [])
    for d in (1, 2, 3):
        m_z[d].wait_recv()
    dz_b = norm_back(1, grad, summed(0, copies))
    slabs = wbuf.shape[0] // 4
    chunk = half // 2

    def back(dz, core, c, lane):
        part = wbuf[pl.ds((core * 2 + c) * slabs, slabs)].reshape(chunk, cols)
        group = lax.broadcasted_iota(jnp.int32, (1, chunk), 1) + (core * 2 + c) * chunk
        group = (group // (width // GROUPS)).astype(F32)
        return jnp.where(group != ids[:, lane : lane + 1], contract_last(dz, part), 0.0)

    order = [(1 - t, 0), (1 - t, 1), (t, 0), (t, 1)]
    gram_share(1, along_b, within_b)
    for i, (core, c) in enumerate(order[:2]):
        fown[i] = back(dz_b, core, c, 64)
    for copy in within_b:
        copy.wait_recv()
    for d in (1, 2, 3):
        small_z[d].wait_recv()
    power = small[0, 1:2]
    for i in range(1, ZS):
        power = power + small[i, 1:2]
        diag_out[0:1, i * cols : (i + 1) * cols] = small[i, 0:1]
    diag_out[0:1, 0:cols] = small[0, 0:1]
    grad, copies = grad_of(0, 1, [power])
    for i, (core, c) in enumerate(order[2:]):
        fown[2 + i] = back(dz_b, core, c, 64)
    total = summed(1, copies)
    last[0] = total
    last_copy = push(last.at[0], last.at[1], sibling)
    dz_a = norm_back(0, grad, total)

    f_s, f_z = {}, {}
    for c in range(2):
        fsib_out[c] = (fown[c] + back(dz_a, 1 - t, c, 0)).astype(BF).reshape(ZS, rows, chunk)
        f_s[c] = push(fsib_out.at[c], fsib.at[c], sibling)
    for c in range(2):
        pair = fown[2 + c] + back(dz_a, t, c, 0)
        f_s[c].wait_recv()
        fown[2 + c] = pair + fsib[c].astype(F32).reshape(many, chunk)
        for d in (2, 1, 3):
            fsend[c, d - 1] = fown[2 + c, block(other_z[d])].astype(BF)
            f_z[c, d] = push(fsend.at[c, d - 1], frecv.at[c, d - 1], at_z[d])
    last_copy.wait_recv()
    power = last[0, 2:3, 0:1] + last[1, 2:3, 0:1]
    cross_out[...] = power / (batch * batch) / emb
    for c in range(2):
        result = fown[2 + c, own]
        for d in (1, 3, 2):
            f_z[c, d].wait_recv()
            result = result + frecv[c, d - 1].astype(F32)
        out[:, c * chunk : (c + 1) * chunk] = LOSS_SCALE * result
    for copy in started:
        copy.wait_send()
    for v in range(2):
        for source in sources:
            hop_on(v, source, lambda copy: copy.wait_send())


COPIES = 128


def fused(feats, jitter, mask_ids, proj_weight):
    rows, width = feats.shape
    depth, local = proj_weight.shape
    cols, half, many = local // ZS, width // 2, rows * ZS
    batch = many * QS
    vmem = pl.BlockSpec(memory_space=pltpu.VMEM)
    grad, diag, power = pl.pallas_call(
        functools.partial(fused_kernel, emb=EMB),
        out_shape=(
            jax.ShapeDtypeStruct((rows, half), F32),
            jax.ShapeDtypeStruct((1, local), F32),
            jax.ShapeDtypeStruct((1, 1), F32),
        ),
        in_specs=[vmem] * 4,
        out_specs=(vmem,) * 3,
        scratch_shapes=[
            pltpu.VMEM((2, many, width), BF),
            pltpu.VMEM((many, 128), F32),
            pltpu.VMEM((ZS * QS, depth, cols), BF),
            pltpu.VMEM((2, QS, many, cols), BF),
            pltpu.VMEM((2, QS, many, cols), BF),
            pltpu.VMEM((2, 2, ZS, rows // 2, batch), BF),
            pltpu.VMEM((2, ZS, rows // 2, batch), BF),
            pltpu.VMEM((2, ZS - 1, rows // 2, batch), BF),
            pltpu.VMEM((2, ZS - 1, rows // 2, batch), BF),
            pltpu.VMEM((2, rows // 2, batch), F32),
            pltpu.VMEM((2, ZS, 2, rows // 2, batch), BF),
            pltpu.VMEM((2, QS, 8, cols), F32),
            pltpu.VMEM((ZS, 8, cols), F32),
            pltpu.VMEM((2, QS, 8, cols), F32),
            pltpu.VMEM((2, 8, cols), F32),
            pltpu.VMEM((2, ZS, rows, half // 2), BF),
            pltpu.VMEM((2, ZS, rows, half // 2), BF),
            pltpu.VMEM((4, many, half // 2), F32),
            pltpu.VMEM((2, ZS - 1, rows, half // 2), BF),
            pltpu.VMEM((2, ZS - 1, rows, half // 2), BF),
            pltpu.SemaphoreType.DMA((COPIES,)),
            pltpu.SemaphoreType.DMA((COPIES,)),
            pltpu.SemaphoreType.DMA((2, 2, ZS)),
            pltpu.SemaphoreType.DMA((2, ZS)),
        ],
        compiler_params=pltpu.CompilerParams(
            collective_id=0, has_side_effects=True, vmem_limit_bytes=56 * 2**20
        ),
    )(feats, jitter, mask_ids.T, proj_weight)
    return grad, diag.reshape(local), power.reshape(())


def solution(mesh):
    in_specs = (P("dp", None), P("dp", None), P("dp", None), P("dp", "tile"))
    out_specs = (P("dp", "tile"), P("tile"), P())
    planes = mesh.shape["dp"] == ZS * QS and mesh.shape["tile"] == 2
    return jax.shard_map(
        fused if planes else on_device, mesh=mesh, in_specs=in_specs, out_specs=out_specs, check_vma=False
    )
```
